512 devices in a mesh: angle: 16 (over z, core), tx: 4 (over y_hi), ty: 8 (over y_lo, x).
Axes of the slice: x: 4, y: 8 (y_hi: 4, y_lo: 2; y = y_hi * 2 + y_lo), z: 8, core: 2. Of those that a mesh axis runs over, the one named last changes fastest.
Arguments:
- index: float32 [64, 512, 512], P('angle', 'ty', 'tx'), may hold values from -6 to 6
- measured: float32 [2, 16, 512, 512], P(None, 'angle', 'ty', 'tx'), may hold values from -6 to 6
- illum: int32 [16, 2], P('angle'), may hold values from -16 to 16
Outputs:
- gradient: float32 [64, 512, 512], P('angle', 'ty', 'tx')
- index_new: float32 [64, 512, 512], P('angle', 'ty', 'tx')
The draws below stay inside these ranges and needn't reach their ends.
All inputs are finite; a program needn't handle non-finite values.
Results may differ from the reference program's by a relative error of at most 0.000054.
Values sent between devices are 32-bit elements; how exact they have to be, the bound alone decides.
No kernel may reach another device: no remote copies, remote signals or barrier semaphores. Data moves between devices by JAX's collectives and lax.ppermute only.
A program may use at most 64 MiB of HBM per device.

```python
import math
import jax
import jax.numpy as jnp
from jax import lax

NX = 512
NY = 512
TV_STEPS = 3
NZ = 64
ANGLES = 16


def draw_measured(key, part):
    key = jax.random.fold_in(key, 11)
    k_rough, k_fx, k_fy, k_amp, k_phase = jax.random.split(key, 5)
    waves = 6
    top = max(1, NX // 64)
    top_y = max(1, NY // 64)
    wave_shape = (2, ANGLES, waves)
    freq_x = jax.random.randint(k_fx, wave_shape, -top, top + 1).astype(jnp.float32)
    freq_y = jax.random.randint(k_fy, wave_shape, -top_y, top_y + 1).astype(jnp.float32)
    offset = jax.random.uniform(k_phase, wave_shape, jnp.float32, -math.pi, math.pi)
    xs = jnp.arange(NX, dtype=jnp.float32)[None, None, None, :]
    ys = jnp.arange(NY, dtype=jnp.float32)[None, None, :, None]
    amps = jax.random.uniform(k_amp, wave_shape, jnp.float32, 0.3, 0.6)
    rough = 0.6 * jax.random.truncated_normal(k_rough, -4.0, 4.0, (2, ANGLES, NY, NX), jnp.float32)
    smooth = jnp.zeros((2, ANGLES, NY, NX), jnp.float32)
    for which in range(waves):
        angle_w = 2.0 * math.pi * (freq_x[:, :, which, None, None] * xs / NX + freq_y[:, :, which, None, None] * ys / NY)
        smooth = smooth + amps[:, :, which, None, None] * jnp.cos(angle_w + offset[:, :, which, None, None])
    return smooth + rough


def place_ends(drawn, own_key, smallest, largest):
    extent = drawn.shape
    place = [jax.random.randint(jax.random.fold_in(own_key, axis), (), 0, extent[axis]) for axis in range(len(extent))]
    drawn = drawn.at[tuple(place)].set(smallest)
    longest = extent.index(max(extent))
    place[longest] = (place[longest] + 1) % extent[longest]
    return drawn.at[tuple(place)].set(largest)


def level_of(rng, extent, shards, smallest, high):
    loudness, own = 1.0, jax.random.fold_in(rng, 6)
    for axis_at, blocks in shards:
        steps = jnp.exp(jax.random.uniform(jax.random.fold_in(own, axis_at), (blocks,), jnp.float32, smallest / len(shards), high / len(shards)))
        loudness = loudness * jnp.repeat(steps, extent[axis_at] // blocks).reshape([-1 if axis == axis_at else 1 for axis in range(len(extent))])
    return loudness


def bell_draw(stream_key, shape, scale, bound, cuts=(), kind=jnp.bfloat16):
    gain = level_of(stream_key, shape, cuts, -0.22, 0.18) if cuts else 1.0
    result = jax.random.normal(stream_key, shape, jnp.float32) * scale * gain
    return jnp.minimum(jnp.maximum(result, -bound), bound).astype(kind)


def setup_inputs(seed: int = 0) -> dict:
    key_of = jax.random.split(jax.random.key(seed), 4)
    return {
        "index": bell_draw(key_of[0], (NZ, NY, NX), 1.0, 6.0, ((0, 16), (1, 8), (2, 4)), jnp.float32),
        "measured": draw_measured(jax.random.fold_in(key_of[3], 71), 0),
        "illum": place_ends(jax.random.randint(key_of[2], (ANGLES, 2), -16, 17), jax.random.fold_in(key_of[2], 1), -16, 16).astype(jnp.int32),
    }


damping = 0.2
disperse = 0.1
phase_scale = 0.1
step_size = 0.1
tv_rate = 0.05
tv_smooth = 0.1

def laplace(field):
    return jnp.roll(field, 1, -1) + jnp.roll(field, -1, -1) + jnp.roll(field, 1, -2) + jnp.roll(field, -1, -2) - 4.0 * field

def exit_loss(volume, wave_in, target):

    def slice_step(field, layer):
        lap = laplace(field)
        wre = field[0] + damping * lap[0] - disperse * lap[1]
        wim = field[1] + damping * lap[1] + disperse * lap[0]
        phase = phase_scale * layer
        cosine = jnp.cos(phase)
        sine = jnp.sin(phase)
        return (jnp.stack([cosine * wre - sine * wim, cosine * wim + sine * wre]), None)
    field, _ = lax.scan(slice_step, wave_in, volume)
    diff = field - target
    return 0.5 * jnp.sum(diff * diff)

def tv_once(volume):
    depth_pos = jnp.arange(volume.shape[0])[:, None, None]
    diff_z = jnp.roll(volume, -1, 0) - volume
    diff_z = jnp.where(depth_pos == volume.shape[0] - 1, 0.0, diff_z)
    diff_y = jnp.roll(volume, -1, 1) - volume
    diff_x = jnp.roll(volume, -1, 2) - volume
    magnitude = jnp.sqrt(diff_z * diff_z + diff_y * diff_y + diff_x * diff_x + tv_smooth * tv_smooth)
    flux_z = diff_z / magnitude
    flux_y = diff_y / magnitude
    flux_x = diff_x / magnitude
    divergence = flux_z - jnp.roll(flux_z, 1, 0) + flux_y - jnp.roll(flux_y, 1, 1) + flux_x - jnp.roll(flux_x, 1, 2)
    return volume + tv_rate * divergence

def reference(index, measured, illum):
    xs = jnp.arange(NX, dtype=jnp.float32)
    ys = jnp.arange(NY, dtype=jnp.float32)
    grad_fn = jax.grad(exit_loss)

    def per_angle(total, item):
        pair, target = item
        freq_x = pair[0].astype(jnp.float32)
        freq_y = pair[1].astype(jnp.float32)
        angle_q = 2.0 * math.pi * (freq_x * xs[None, :] / NX + freq_y * ys[:, None] / NY)
        wave = jnp.stack([jnp.cos(angle_q), jnp.sin(angle_q)])
        return (total + grad_fn(index, wave, target), None)
    start = jnp.zeros(index.shape, jnp.float32)
    gradient, _ = lax.scan(per_angle, start, (illum, jnp.moveaxis(measured, 1, 0)))
    volume = index - step_size * gradient
    for turn in range(TV_STEPS):
        volume = tv_once(volume)
    return (gradient, volume)
```

```python
import functools
import math

import jax
import jax.numpy as jnp
import numpy as np
from jax import lax
from jax.experimental import pallas as pl
from jax.experimental.pallas import tpu as pltpu
from jax.sharding import PartitionSpec as P

TV_STEPS = 3
HALO = 64
GROUP = 8

damping = 0.2
disperse = 0.1
phase_scale = 0.1
step_size = 0.1
tv_rate = 0.05
tv_smooth = 0.1

SPREAD = complex(damping, disperse)
GAIN = abs(SPREAD)
TURN = SPREAD / GAIN


def _fit():
    nodes = np.cos((np.arange(400) + 0.5) * np.pi / 400)
    t = 3.05 * (nodes + 1.0)
    z = t * t
    scaled = z / z.max()
    even = np.linalg.lstsq(scaled[:, None] ** np.arange(5), GAIN * np.cos(phase_scale * t), rcond=None)[0]
    odd = np.linalg.lstsq(scaled[:, None] ** np.arange(5), GAIN * np.sin(phase_scale * t) / t, rcond=None)[0]
    powers = z.max() ** np.arange(5)
    return [float(v) for v in even / powers], [float(v) for v in odd / powers]


EVEN, ODD = _fit()


def phase_factor(t):
    z = t * t
    cosine = EVEN[4]
    for coef in EVEN[3::-1]:
        cosine = cosine * z + coef
    sine = ODD[4]
    for coef in ODD[3::-1]:
        sine = sine * z + coef
    return cosine, sine * t


def neighbours(buf, slot, part, row, first, last):
    mid = [buf[slot, 2 * part + half, pl.ds(row, 8), :] for half in range(2)]
    low = [pltpu.roll(m, 1, 1) for m in mid]
    high = [pltpu.roll(m, 127, 1) for m in mid]
    out = []
    for half in range(2):
        left = jnp.where(first, low[1 - half], low[half])
        right = jnp.where(last, high[1 - half], high[half])
        up = buf[slot, 2 * part + half, pl.ds(row - 1, 8), :]
        down = buf[slot, 2 * part + half, pl.ds(row + 1, 8), :]
        out.append((left + right) + (up + down))
    return mid, out


def lane_masks():
    lane = lax.broadcasted_iota(jnp.int32, (8, 128), 1)
    return lane == 0, lane == 127


def forward_kernel(rows, index_ref, start_ref, field_ref, buf):
    chunks = rows // 8
    pid = pl.program_id(0)
    first, last = lane_masks()

    @pl.when(pid == 0)
    def _():
        buf[...] = jnp.zeros_like(buf)
        for q in range(4):
            buf[0, q, 8 : 8 + rows, :] = start_ref[q // 2, q % 2]

    def step(j, parity, lo, hi):
        for c in range(lo, hi):
            row = 8 + 8 * c
            re, sum_re = neighbours(buf, parity, 0, row, first, last)
            im, sum_im = neighbours(buf, parity, 1, row, first, last)
            for half in range(2):
                cosine, sine = phase_factor(index_ref[j, half, pl.ds(8 * c, 8), :])
                wre = sum_re[half] + (im[half] + im[half])
                wim = sum_im[half] - (re[half] + re[half])
                nre = cosine * wre - sine * wim
                nim = cosine * wim + sine * wre
                buf[1 - parity, half, pl.ds(row, 8), :] = nre
                buf[1 - parity, 2 + half, pl.ds(row, 8), :] = nim
                if half == 0 and chunks // 3 <= c < 2 * chunks // 3:
                    own = 8 * (c - chunks // 3)
                    field_ref[j, 0, pl.ds(own, 8), :] = nre
                    field_ref[j, 1, pl.ds(own, 8), :] = nim

    for k in range(8):

        @pl.when(pid == k)
        def _(k=k):
            @pl.loop(0, GROUP // 2)
            def _(pair):
                step(2 * pair, 0, k, chunks - k)
                step(2 * pair + 1, 1, k, chunks - k)


def backward_kernel(rows, index_ref, start_ref, field_ref, grad_ref, buf):
    chunks = rows // 8
    pid = pl.program_id(0)
    first, last = lane_masks()

    @pl.when(pid == 0)
    def _():
        buf[...] = jnp.zeros_like(buf)

    def finish(j, parity, c, half, are, aim):
        if half == 0 and chunks // 3 <= c < 2 * chunks // 3:
            own = 8 * (c - chunks // 3)
            fre = field_ref[j, 0, pl.ds(own, 8), :]
            fim = field_ref[j, 1, pl.ds(own, 8), :]
            slab = GROUP // 2
            grad_ref[j // slab, 0, j % slab, pl.ds(own, 8), :] = phase_scale * (aim * fre - are * fim)
        cosine, sine = phase_factor(index_ref[j, half, pl.ds(8 * c, 8), :])
        row = 8 + 8 * c
        buf[parity, half, pl.ds(row, 8), :] = cosine * are + sine * aim
        buf[parity, 2 + half, pl.ds(row, 8), :] = cosine * aim - sine * are

    def step(j, parity, lo, hi):
        for c in range(lo, hi):
            row = 8 + 8 * c
            re, sum_re = neighbours(buf, 1 - parity, 0, row, first, last)
            im, sum_im = neighbours(buf, 1 - parity, 1, row, first, last)
            for half in range(2):
                are = sum_re[half] - (im[half] + im[half])
                aim = sum_im[half] + (re[half] + re[half])
                finish(j, parity, c, half, are, aim)

    for k in range(8):

        @pl.when(pid == k)
        def _(k=k):
            skip = 0
            if k == 0:
                skip = 1
                for c in range(chunks):
                    for half in range(2):
                        finish(
                            GROUP - 1,
                            1,
                            c,
                            half,
                            start_ref[0, half, pl.ds(8 * c, 8), :],
                            start_ref[1, half, pl.ds(8 * c, 8), :],
                        )
                step(GROUP - 2, 0, k, chunks - k)

            @pl.loop(skip, GROUP // 2)
            def _(pair):
                step(GROUP - 1 - 2 * pair, 1, k, chunks - k)
                step(GROUP - 2 - 2 * pair, 0, k, chunks - k)


def ring(count, by):
    return [(i, (i + by) % count) for i in range(count)]


def widen(block, axis_x, axis_y):
    n, rows, cols = block.shape
    half = cols // 2
    nx, ny = lax.axis_size(axis_x), lax.axis_size(axis_y)
    pack = lambda v: jnp.concatenate([v[: n // 2], v[n // 2 :]], axis=2)
    unpack = lambda v: jnp.concatenate([v[:, :, :half], v[:, :, half:]], axis=0)
    left = unpack(lax.ppermute(pack(block[:, :, half:]), axis_x, ring(nx, 1)))
    right = unpack(lax.ppermute(pack(block[:, :, :half]), axis_x, ring(nx, -1)))
    wide = jnp.stack([block, jnp.concatenate([right, left], axis=2)], axis=1)
    above = lax.ppermute(wide, axis_y, ring(ny, 1))
    below = lax.ppermute(wide, axis_y, ring(ny, -1))
    return jnp.concatenate([above, wide, below], axis=2)


def with_halo(block, sides, width):
    for axis, dim in sides:
        count = lax.axis_size(axis)
        low = lax.ppermute(
            lax.slice_in_dim(block, block.shape[dim] - width, None, axis=dim), axis, ring(count, 1)
        )
        high = lax.ppermute(lax.slice_in_dim(block, 0, width, axis=dim), axis, ring(count, -1))
        block = jnp.concatenate([low, block, high], axis=dim)
    return block


def smooth(extended, reach, z_first, nz_total):
    length = extended.shape[0]
    base = extended[:-1, :-1, :-1]
    diff_z = extended[1:, :-1, :-1] - base
    diff_y = extended[:-1, 1:, :-1] - base
    diff_x = extended[:-1, :-1, 1:] - base
    depth_pos = (z_first - reach + jnp.arange(length - 1)) % nz_total
    diff_z = jnp.where(depth_pos[:, None, None] == nz_total - 1, 0.0, diff_z)
    scale = lax.rsqrt(
        diff_z * diff_z + diff_y * diff_y + diff_x * diff_x + tv_smooth * tv_smooth
    )
    flux_z = diff_z * scale
    flux_y = diff_y * scale
    flux_x = diff_x * scale
    divergence = (
        flux_z[1:, 1:, 1:]
        - flux_z[:-1, 1:, 1:]
        + flux_y[1:, 1:, 1:]
        - flux_y[1:, :-1, 1:]
        + flux_x[1:, 1:, 1:]
        - flux_x[1:, 1:, :-1]
    )
    return extended[1:-1, 1:-1, 1:-1] + tv_rate * divergence


def body(index, measured, illum):
    slab, rows, cols = index.shape
    depth = lax.axis_size("angle")
    nz = slab * depth
    nx = cols * lax.axis_size("tx")
    ny = rows * lax.axis_size("ty")
    tall = 3 * rows
    core_groups = [[2 * i, 2 * i + 1] for i in range(depth // 2)]
    chip_groups = [list(range(c, depth, 2)) for c in range(2)]

    half = lax.broadcasted_iota(jnp.int32, (2, tall, cols), 0)
    lane = lax.broadcasted_iota(jnp.int32, (2, tall, cols), 2)
    gx = lax.axis_index("tx") * cols + jnp.where(half == 0, lane, jnp.where(lane < cols // 2, lane + cols, lane - cols))
    gy = lax.axis_index("ty") * rows - rows + lax.broadcasted_iota(jnp.int32, (2, tall, cols), 1)
    turns = (illum[0, 0] * gx * (ny // math.gcd(nx, ny)) + illum[0, 1] * gy * (nx // math.gcd(nx, ny)))
    whole = math.lcm(nx, ny)
    turns = lax.rem(lax.rem(turns, whole) + whole, whole)
    q = (2.0 * math.pi / whole) * turns.astype(jnp.float32)
    start = jnp.stack([jnp.cos(q), jnp.sin(q)])

    column = lax.all_gather(widen(index, "tx", "ty"), "angle", axis=0, tiled=True)

    index_block = (GROUP, 2, tall, cols)
    field_block = (GROUP, 2, rows, cols)
    steps = nz // GROUP
    scratch = [pltpu.VMEM((2, 4, tall + 16, cols), jnp.float32)]
    params = pltpu.CompilerParams(dimension_semantics=("arbitrary",), vmem_limit_bytes=40 * 2**20)
    fields = pl.pallas_call(
        functools.partial(forward_kernel, tall),
        grid=(steps,),
        in_specs=[
            pl.BlockSpec(index_block, lambda i: (i, 0, 0, 0)),
            pl.BlockSpec((2, 2, tall, cols), lambda i: (0, 0, 0, 0)),
        ],
        out_specs=pl.BlockSpec(field_block, lambda i: (i, 0, 0, 0)),
        out_shape=jax.ShapeDtypeStruct((nz, 2, rows, cols), jnp.float32),
        scratch_shapes=scratch,
        compiler_params=params,
        name="forward",
    )(column, start)

    back = (TURN.conjugate() ** nz)
    back = back / abs(back)
    target_re = back.real * measured[0] - back.imag * measured[1]
    target_im = back.real * measured[1] + back.imag * measured[0]
    residual = fields[nz - 1] - jnp.concatenate([target_re, target_im], axis=0)
    adjoint = widen(residual, "tx", "ty")

    grads = pl.pallas_call(
        functools.partial(backward_kernel, tall),
        grid=(steps,),
        in_specs=[
            pl.BlockSpec(index_block, lambda i: (steps - 1 - i, 0, 0, 0)),
            pl.BlockSpec((2, 2, tall, cols), lambda i: (0, 0, 0, 0)),
            pl.BlockSpec(field_block, lambda i: (steps - 1 - i, 0, 0, 0)),
        ],
        out_specs=pl.BlockSpec((2, 1, slab, rows, cols), lambda i: (0, steps - 1 - i, 0, 0, 0)),
        out_shape=jax.ShapeDtypeStruct((2, depth // 2, slab, rows, cols), jnp.float32),
        scratch_shapes=scratch,
        compiler_params=params,
        name="backward",
    )(column, adjoint, fields)

    pair = lax.all_to_all(grads, "angle", 0, 0, tiled=True, axis_index_groups=core_groups)
    both = pair[0] + pair[1]
    parts = lax.all_to_all(both, "angle", 0, 0, tiled=True, axis_index_groups=chip_groups)
    gradient = jnp.sum(parts, axis=0)

    volume = index - step_size * gradient
    z_first = lax.axis_index("angle") * slab
    extended = with_halo(volume, (("angle", 0), ("tx", 2), ("ty", 1)), TV_STEPS)
    for turn in range(TV_STEPS):
        extended = smooth(extended, TV_STEPS - turn, z_first, nz)
    return (gradient, extended)


def solution(mesh):
    in_specs = (P("angle", "ty", "tx"), P(None, "angle", "ty", "tx"), P("angle", None))
    out_specs = (P("angle", "ty", "tx"), P("angle", "ty", "tx"))
    return jax.shard_map(body, mesh=mesh, in_specs=in_specs, out_specs=out_specs, check_vma=False)
```

```python
import functools
import math

import jax
import jax.numpy as jnp
import numpy as np
from jax import lax
from jax.experimental import pallas as pl
from jax.experimental.pallas import tpu as pltpu
from jax.sharding import PartitionSpec as P

TV_STEPS = 3
HALO = 64
GROUP = 8

damping = 0.2
disperse = 0.1
phase_scale = 0.1
step_size = 0.1
tv_rate = 0.05
tv_smooth = 0.1

SPREAD = complex(damping, disperse)
GAIN = abs(SPREAD)
TURN = SPREAD / GAIN


def _fit():
    nodes = np.cos((np.arange(400) + 0.5) * np.pi / 400)
    t = 3.05 * (nodes + 1.0)
    z = t * t
    scaled = z / z.max()
    even = np.linalg.lstsq(scaled[:, None] ** np.arange(4), GAIN * np.cos(phase_scale * t), rcond=None)[0]
    odd = np.linalg.lstsq(scaled[:, None] ** np.arange(4), GAIN * np.sin(phase_scale * t) / t, rcond=None)[0]
    powers = z.max() ** np.arange(4)
    return [float(v) for v in even / powers], [float(v) for v in odd / powers]


EVEN, ODD = _fit()


def phase_factor(t):
    z = t * t
    cosine = EVEN[3]
    for coef in EVEN[2::-1]:
        cosine = cosine * z + coef
    sine = ODD[3]
    for coef in ODD[2::-1]:
        sine = sine * z + coef
    return cosine, sine * t


def neighbours(buf, slot, part, row, first, last):
    mid = [buf[slot, 2 * part + half, pl.ds(row, 8), :] for half in range(2)]
    low = [pltpu.roll(m, 1, 1) for m in mid]
    high = [pltpu.roll(m, 127, 1) for m in mid]
    out = []
    for half in range(2):
        left = jnp.where(first, low[1 - half], low[half])
        right = jnp.where(last, high[1 - half], high[half])
        up = buf[slot, 2 * part + half, pl.ds(row - 1, 8), :]
        down = buf[slot, 2 * part + half, pl.ds(row + 1, 8), :]
        out.append((left + right) + (up + down))
    return mid, out


def index_rows(index_ref, j, half, c, chunks):
    third = chunks // 3
    if half == 0:
        return index_ref[j, pl.ds(8 * c, 8), :]
    if c < third:
        return index_ref[j, pl.ds(8 * (4 * third + c), 8), :]
    if c < 2 * third:
        return index_ref[j, pl.ds(8 * (2 * third + c), 8), :]
    return pltpu.roll(index_ref[j, pl.ds(8 * (2 * third + c), 8), :], 64, 1)


def lane_masks():
    lane = lax.broadcasted_iota(jnp.int32, (8, 128), 1)
    return lane == 0, lane == 127


def forward_kernel(rows, index_ref, start_ref, field_ref, buf):
    chunks = rows // 8
    pid = pl.program_id(0)
    first, last = lane_masks()

    @pl.when(pid == 0)
    def _():
        buf[...] = jnp.zeros_like(buf)
        for q in range(4):
            buf[0, q, 8 : 8 + rows, :] = start_ref[q // 2, q % 2]

    def step(j, parity, lo, hi):
        for c in range(lo, hi):
            row = 8 + 8 * c
            re, sum_re = neighbours(buf, parity, 0, row, first, last)
            im, sum_im = neighbours(buf, parity, 1, row, first, last)
            for half in range(2):
                cosine, sine = phase_factor(index_rows(index_ref, j, half, c, chunks))
                wre = sum_re[half] + (im[half] + im[half])
                wim = sum_im[half] - (re[half] + re[half])
                nre = cosine * wre - sine * wim
                nim = cosine * wim + sine * wre
                buf[1 - parity, half, pl.ds(row, 8), :] = nre
                buf[1 - parity, 2 + half, pl.ds(row, 8), :] = nim
                if half == 0 and chunks // 3 <= c < 2 * chunks // 3:
                    own = 8 * (c - chunks // 3)
                    field_ref[j, 0, pl.ds(own, 8), :] = nre
                    field_ref[j, 1, pl.ds(own, 8), :] = nim

    for k in range(8):

        @pl.when(pid == k)
        def _(k=k):
            @pl.loop(0, GROUP // 2)
            def _(pair):
                step(2 * pair, 0, k, chunks - k)
                step(2 * pair + 1, 1, k, chunks - k)


def backward_kernel(rows, index_ref, start_ref, field_ref, grad_ref, buf):
    chunks = rows // 8
    pid = pl.program_id(0)
    first, last = lane_masks()

    @pl.when(pid == 0)
    def _():
        buf[...] = jnp.zeros_like(buf)

    def finish(j, parity, c, half, are, aim):
        if half == 0 and chunks // 3 <= c < 2 * chunks // 3:
            own = 8 * (c - chunks // 3)
            fre = field_ref[j, 0, pl.ds(own, 8), :]
            fim = field_ref[j, 1, pl.ds(own, 8), :]
            slab = GROUP // 2
            grad_ref[j // slab, 0, j % slab, pl.ds(own, 8), :] = phase_scale * (aim * fre - are * fim)
        cosine, sine = phase_factor(index_rows(index_ref, j, half, c, chunks))
        row = 8 + 8 * c
        buf[parity, half, pl.ds(row, 8), :] = cosine * are + sine * aim
        buf[parity, 2 + half, pl.ds(row, 8), :] = cosine * aim - sine * are

    def step(j, parity, lo, hi):
        for c in range(lo, hi):
            row = 8 + 8 * c
            re, sum_re = neighbours(buf, 1 - parity, 0, row, first, last)
            im, sum_im = neighbours(buf, 1 - parity, 1, row, first, last)
            for half in range(2):
                are = sum_re[half] - (im[half] + im[half])
                aim = sum_im[half] + (re[half] + re[half])
                finish(j, parity, c, half, are, aim)

    for k in range(8):

        @pl.when(pid == k)
        def _(k=k):
            skip = 0
            if k == 0:
                skip = 1
                for c in range(chunks):
                    for half in range(2):
                        finish(
                            GROUP - 1,
                            1,
                            c,
                            half,
                            start_ref[0, half, pl.ds(8 * c, 8), :],
                            start_ref[1, half, pl.ds(8 * c, 8), :],
                        )
                step(GROUP - 2, 0, k, chunks - k)

            @pl.loop(skip, GROUP // 2)
            def _(pair):
                step(GROUP - 1 - 2 * pair, 1, k, chunks - k)
                step(GROUP - 2 - 2 * pair, 0, k, chunks - k)


def ring(count, by):
    return [(i, (i + by) % count) for i in range(count)]


def widen(block, axis_x, axis_y):
    n, rows, cols = block.shape
    half = cols // 2
    nx, ny = lax.axis_size(axis_x), lax.axis_size(axis_y)
    pack = lambda v: jnp.concatenate([v[: n // 2], v[n // 2 :]], axis=2)
    unpack = lambda v: jnp.concatenate([v[:, :, :half], v[:, :, half:]], axis=0)
    left = unpack(lax.ppermute(pack(block[:, :, half:]), axis_x, ring(nx, 1)))
    right = unpack(lax.ppermute(pack(block[:, :, :half]), axis_x, ring(nx, -1)))
    wide = jnp.stack([block, jnp.concatenate([right, left], axis=2)], axis=1)
    above = lax.ppermute(wide, axis_y, ring(ny, 1))
    below = lax.ppermute(wide, axis_y, ring(ny, -1))
    return above, wide, below


def pack_corners(above, wide, below):
    _, _, rows, cols = wide.shape
    lane = lax.broadcasted_iota(jnp.int32, (rows, cols), 1)
    away = jnp.where(lane < cols // 2, lane + 1, cols - lane)
    from_above = away <= lax.broadcasted_iota(jnp.int32, (rows, cols), 0)
    corners = jnp.where(from_above, above[:, 1], jnp.roll(below[:, 1], cols // 2, axis=2))
    return jnp.concatenate([above[:, 0], wide[:, 0], below[:, 0], wide[:, 1], corners], axis=1)


def with_halo(block, sides, width):
    for axis, dim in sides:
        count = lax.axis_size(axis)
        low = lax.ppermute(
            lax.slice_in_dim(block, block.shape[dim] - width, None, axis=dim), axis, ring(count, 1)
        )
        high = lax.ppermute(lax.slice_in_dim(block, 0, width, axis=dim), axis, ring(count, -1))
        block = jnp.concatenate([low, block, high], axis=dim)
    return block


def smooth(extended, reach, z_first, nz_total):
    length = extended.shape[0]
    base = extended[:-1, :-1, :-1]
    diff_z = extended[1:, :-1, :-1] - base
    diff_y = extended[:-1, 1:, :-1] - base
    diff_x = extended[:-1, :-1, 1:] - base
    depth_pos = (z_first - reach + jnp.arange(length - 1)) % nz_total
    diff_z = jnp.where(depth_pos[:, None, None] == nz_total - 1, 0.0, diff_z)
    scale = lax.rsqrt(
        diff_z * diff_z + diff_y * diff_y + diff_x * diff_x + tv_smooth * tv_smooth
    )
    flux_z = diff_z * scale
    flux_y = diff_y * scale
    flux_x = diff_x * scale
    divergence = (
        flux_z[1:, 1:, 1:]
        - flux_z[:-1, 1:, 1:]
        + flux_y[1:, 1:, 1:]
        - flux_y[1:, :-1, 1:]
        + flux_x[1:, 1:, 1:]
        - flux_x[1:, 1:, :-1]
    )
    return extended[1:-1, 1:-1, 1:-1] + tv_rate * divergence


def body(index, measured, illum):
    slab, rows, cols = index.shape
    depth = lax.axis_size("angle")
    nz = slab * depth
    nx = cols * lax.axis_size("tx")
    ny = rows * lax.axis_size("ty")
    tall = 3 * rows
    core_groups = [[2 * i, 2 * i + 1] for i in range(depth // 2)]
    chip_groups = [list(range(c, depth, 2)) for c in range(2)]

    half = lax.broadcasted_iota(jnp.int32, (2, tall, cols), 0)
    lane = lax.broadcasted_iota(jnp.int32, (2, tall, cols), 2)
    gx = lax.axis_index("tx") * cols + jnp.where(half == 0, lane, jnp.where(lane < cols // 2, lane + cols, lane - cols))
    gy = lax.axis_index("ty") * rows - rows + lax.broadcasted_iota(jnp.int32, (2, tall, cols), 1)
    turns = (illum[0, 0] * gx * (ny // math.gcd(nx, ny)) + illum[0, 1] * gy * (nx // math.gcd(nx, ny)))
    whole = math.lcm(nx, ny)
    turns = lax.rem(lax.rem(turns, whole) + whole, whole)
    q = (2.0 * math.pi / whole) * turns.astype(jnp.float32)
    start = jnp.stack([jnp.cos(q), jnp.sin(q)])

    column = lax.all_gather(pack_corners(*widen(index, "tx", "ty")), "angle", axis=0, tiled=True)

    index_block = (GROUP, 5 * rows, cols)
    field_block = (GROUP, 2, rows, cols)
    steps = nz // GROUP
    scratch = [pltpu.VMEM((2, 4, tall + 16, cols), jnp.float32)]
    params = pltpu.CompilerParams(dimension_semantics=("arbitrary",), vmem_limit_bytes=40 * 2**20)
    fields = pl.pallas_call(
        functools.partial(forward_kernel, tall),
        grid=(steps,),
        in_specs=[
            pl.BlockSpec(index_block, lambda i: (i, 0, 0)),
            pl.BlockSpec((2, 2, tall, cols), lambda i: (0, 0, 0, 0)),
        ],
        out_specs=pl.BlockSpec(field_block, lambda i: (i, 0, 0, 0)),
        out_shape=jax.ShapeDtypeStruct((nz, 2, rows, cols), jnp.float32),
        scratch_shapes=scratch,
        compiler_params=params,
        name="forward",
    )(column, start)

    back = (TURN.conjugate() ** nz)
    back = back / abs(back)
    target_re = back.real * measured[0] - back.imag * measured[1]
    target_im = back.real * measured[1] + back.imag * measured[0]
    residual = fields[nz - 1] - jnp.concatenate([target_re, target_im], axis=0)
    adjoint = jnp.concatenate(widen(residual, "tx", "ty"), axis=2)

    grads = pl.pallas_call(
        functools.partial(backward_kernel, tall),
        grid=(steps,),
        in_specs=[
            pl.BlockSpec(index_block, lambda i: (steps - 1 - i, 0, 0)),
            pl.BlockSpec((2, 2, tall, cols), lambda i: (0, 0, 0, 0)),
            pl.BlockSpec(field_block, lambda i: (steps - 1 - i, 0, 0, 0)),
        ],
        out_specs=pl.BlockSpec((2, 1, slab, rows, cols), lambda i: (0, steps - 1 - i, 0, 0, 0)),
        out_shape=jax.ShapeDtypeStruct((2, depth // 2, slab, rows, cols), jnp.float32),
        scratch_shapes=scratch,
        compiler_params=params,
        name="backward",
    )(column, adjoint, fields)

    pair = lax.all_to_all(grads, "angle", 0, 0, tiled=True, axis_index_groups=core_groups)
    both = pair[0] + pair[1]
    parts = lax.all_to_all(both, "angle", 0, 0, tiled=True, axis_index_groups=chip_groups)
    gradient = jnp.sum(parts, axis=0)

    volume = index - step_size * gradient
    z_first = lax.axis_index("angle") * slab
    extended = with_halo(volume, (("angle", 0), ("tx", 2), ("ty", 1)), TV_STEPS)
    for turn in range(TV_STEPS):
        extended = smooth(extended, TV_STEPS - turn, z_first, nz)
    return (gradient, extended)


def solution(mesh):
    in_specs = (P("angle", "ty", "tx"), P(None, "angle", "ty", "tx"), P("angle", None))
    out_specs = (P("angle", "ty", "tx"), P("angle", "ty", "tx"))
    return jax.shard_map(body, mesh=mesh, in_specs=in_specs, out_specs=out_specs, check_vma=False)
```

```python
import functools
import math

import jax
import jax.numpy as jnp
import numpy as np
from jax import lax
from jax.experimental import pallas as pl
from jax.experimental.pallas import tpu as pltpu
from jax.sharding import PartitionSpec as P

TV_STEPS = 3
HALO = 64
GROUP = 8

damping = 0.2
disperse = 0.1
phase_scale = 0.1
step_size = 0.1
tv_rate = 0.05
tv_smooth = 0.1

SPREAD = complex(damping, disperse)
GAIN = abs(SPREAD)
TURN = SPREAD / GAIN


def _fit():
    nodes = np.cos((np.arange(400) + 0.5) * np.pi / 400)
    t = 3.05 * (nodes + 1.0)
    z = t * t
    scaled = z / z.max()
    even = np.linalg.lstsq(scaled[:, None] ** np.arange(4), GAIN * np.cos(phase_scale * t), rcond=None)[0]
    odd = np.linalg.lstsq(scaled[:, None] ** np.arange(4), GAIN * np.sin(phase_scale * t) / t, rcond=None)[0]
    powers = z.max() ** np.arange(4)
    return [float(v) for v in even / powers], [float(v) for v in odd / powers]


EVEN, ODD = _fit()


def phase_factor(t):
    z = t * t
    cosine = EVEN[3]
    for coef in EVEN[2::-1]:
        cosine = cosine * z + coef
    sine = ODD[3]
    for coef in ODD[2::-1]:
        sine = sine * z + coef
    return cosine, sine * t


def neighbours(buf, slot, part, row, first, last):
    mid = [buf[slot, 2 * part + half, pl.ds(row, 8), :] for half in range(2)]
    low = [pltpu.roll(m, 1, 1) for m in mid]
    high = [pltpu.roll(m, 127, 1) for m in mid]
    out = []
    for half in range(2):
        left = jnp.where(first, low[1 - half], low[half])
        right = jnp.where(last, high[1 - half], high[half])
        up = buf[slot, 2 * part + half, pl.ds(row - 1, 8), :]
        down = buf[slot, 2 * part + half, pl.ds(row + 1, 8), :]
        out.append((left + right) + (up + down))
    return mid, out


def index_rows(index_ref, j, half, c, chunks):
    third = chunks // 3
    if half == 0:
        return index_ref[j, pl.ds(8 * c, 8), :]
    if c < third:
        return index_ref[j, pl.ds(8 * (4 * third + c), 8), :]
    if c < 2 * third:
        return index_ref[j, pl.ds(8 * (2 * third + c), 8), :]
    return pltpu.roll(index_ref[j, pl.ds(8 * (2 * third + c), 8), :], 64, 1)


def lane_masks():
    lane = lax.broadcasted_iota(jnp.int32, (8, 128), 1)
    return lane == 0, lane == 127


def forward_kernel(rows, index_ref, start_ref, field_ref, buf):
    chunks = rows // 8
    pid = pl.program_id(0)
    first, last = lane_masks()

    @pl.when(pid == 0)
    def _():
        buf[...] = jnp.zeros_like(buf)
        for q in range(4):
            buf[0, q, 8 : 8 + rows, :] = start_ref[q // 2, q % 2]

    def step(j, parity, lo, hi):
        for c in range(lo, hi):
            row = 8 + 8 * c
            re, sum_re = neighbours(buf, parity, 0, row, first, last)
            im, sum_im = neighbours(buf, parity, 1, row, first, last)
            for half in range(2):
                cosine, sine = phase_factor(index_rows(index_ref, j, half, c, chunks))
                wre = sum_re[half] + (im[half] + im[half])
                wim = sum_im[half] - (re[half] + re[half])
                nre = cosine * wre - sine * wim
                nim = cosine * wim + sine * wre
                buf[1 - parity, half, pl.ds(row, 8), :] = nre
                buf[1 - parity, 2 + half, pl.ds(row, 8), :] = nim
                if half == 0 and chunks // 3 <= c < 2 * chunks // 3:
                    own = 8 * (c - chunks // 3)
                    field_ref[j, 0, pl.ds(own, 8), :] = nre
                    field_ref[j, 1, pl.ds(own, 8), :] = nim

    for k in range(8):

        @pl.when(pid == k)
        def _(k=k):
            @pl.loop(0, GROUP // 2)
            def _(pair):
                step(2 * pair, 0, k, chunks - k)
                step(2 * pair + 1, 1, k, chunks - k)


def backward_kernel(rows, index_ref, start_ref, field_ref, grad_ref, buf):
    chunks = rows // 8
    pid = pl.program_id(0)
    first, last = lane_masks()

    @pl.when(pid == 0)
    def _():
        buf[...] = jnp.zeros_like(buf)

    def finish(j, parity, c, half, are, aim):
        if half == 0 and chunks // 3 <= c < 2 * chunks // 3:
            own = 8 * (c - chunks // 3)
            fre = field_ref[j, 0, pl.ds(own, 8), :]
            fim = field_ref[j, 1, pl.ds(own, 8), :]
            slab = GROUP // 2
            grad_ref[j // slab, 0, j % slab, pl.ds(own, 8), :] = phase_scale * (aim * fre - are * fim)
        cosine, sine = phase_factor(index_rows(index_ref, j, half, c, chunks))
        row = 8 + 8 * c
        buf[parity, half, pl.ds(row, 8), :] = cosine * are + sine * aim
        buf[parity, 2 + half, pl.ds(row, 8), :] = cosine * aim - sine * are

    def step(j, parity, lo, hi):
        for c in range(lo, hi):
            row = 8 + 8 * c
            re, sum_re = neighbours(buf, 1 - parity, 0, row, first, last)
            im, sum_im = neighbours(buf, 1 - parity, 1, row, first, last)
            for half in range(2):
                are = sum_re[half] - (im[half] + im[half])
                aim = sum_im[half] + (re[half] + re[half])
                finish(j, parity, c, half, are, aim)

    for k in range(8):

        @pl.when(pid == k)
        def _(k=k):
            skip = 0
            if k == 0:
                skip = 1
                for c in range(chunks):
                    for half in range(2):
                        finish(
                            GROUP - 1,
                            1,
                            c,
                            half,
                            start_ref[0, half, pl.ds(8 * c, 8), :],
                            start_ref[1, half, pl.ds(8 * c, 8), :],
                        )
                step(GROUP - 2, 0, k, chunks - k)

            @pl.loop(skip, GROUP // 2)
            def _(pair):
                step(GROUP - 1 - 2 * pair, 1, k, chunks - k)
                step(GROUP - 2 - 2 * pair, 0, k, chunks - k)


def ring(count, by):
    return [(i, (i + by) % count) for i in range(count)]


def widen(block, axis_x, axis_y):
    n, rows, cols = block.shape
    half = cols // 2
    nx, ny = lax.axis_size(axis_x), lax.axis_size(axis_y)
    pack = lambda v: jnp.concatenate([v[: n // 2], v[n // 2 :]], axis=2)
    unpack = lambda v: jnp.concatenate([v[:, :, :half], v[:, :, half:]], axis=0)
    left = unpack(lax.ppermute(pack(block[:, :, half:]), axis_x, ring(nx, 1)))
    right = unpack(lax.ppermute(pack(block[:, :, :half]), axis_x, ring(nx, -1)))
    wide = jnp.stack([block, jnp.concatenate([right, left], axis=2)], axis=1)
    above = lax.ppermute(wide, axis_y, ring(ny, 1))
    below = lax.ppermute(wide, axis_y, ring(ny, -1))
    return above, wide, below


def pack_corners(above, wide, below):
    _, _, rows, cols = wide.shape
    lane = lax.broadcasted_iota(jnp.int32, (rows, cols), 1)
    away = jnp.where(lane < cols // 2, lane + 1, cols - lane)
    from_above = away <= lax.broadcasted_iota(jnp.int32, (rows, cols), 0)
    corners = jnp.where(from_above, above[:, 1], jnp.roll(below[:, 1], cols // 2, axis=2))
    return jnp.concatenate([above[:, 0], wide[:, 0], below[:, 0], wide[:, 1], corners], axis=1)


AROUND = [(0, -1), (0, 1), (1, -1), (1, 0), (1, 1), (-1, -1), (-1, 0), (-1, 1)]
STRIDE = 4


def tile_at(nx, ny, dx, dy):
    tx, ty = lax.axis_index("tx"), lax.axis_index("ty")
    return lax.rem(tx + dx + nx, nx) * ny + lax.rem(ty + dy + ny, ny)


def share_kernel(nx, ny, parts_ref, index_ref, grad_ref, vol_ref, out_ref):
    slab, rows, cols = index_ref.shape
    out_ref[...] = jnp.zeros_like(out_ref)
    for s in range(slab):
        grad = parts_ref[0, s]
        for p in range(1, parts_ref.shape[0]):
            grad = grad + parts_ref[p, s]
        vol = index_ref[s] - step_size * grad
        grad_ref[s] = grad
        vol_ref[s] = vol
        turned = vol.T
        keep = pl.ds(STRIDE * s, TV_STEPS)
        for dx, dy in AROUND:
            spot = tile_at(nx, ny, dx, dy)
            if dx == 0:
                out_ref[spot, keep, :] = vol[rows - TV_STEPS :] if dy > 0 else vol[:TV_STEPS]
            else:
                out_ref[spot, keep, :rows] = turned[cols - TV_STEPS :] if dx > 0 else turned[:TV_STEPS]


def sort_kernel(nx, ny, strips_ref, vol_ref, near_ref, up_ref, down_ref):
    slab, rows, cols = vol_ref.shape
    body_rows = TV_STEPS * rows
    part = STRIDE * TV_STEPS
    for s in range(TV_STEPS):
        down_ref[pl.ds(rows * s, rows), :] = vol_ref[s]
        up_ref[pl.ds(rows * s, rows), :] = vol_ref[slab - TV_STEPS + s]
    for i, (dx, dy) in enumerate(AROUND):
        strip = strips_ref[tile_at(nx, ny, dx, dy)]
        near_ref[i] = strip
        down_ref[pl.ds(body_rows + part * i, part), :] = strip[:part]
        up_ref[pl.ds(body_rows + part * i, part), :] = strip[STRIDE * (slab - TV_STEPS) :]


def smooth_kernel(nz, vol_ref, near_ref, low_ref, high_ref, out_ref, v, fz, fy, fx, turn):
    slab, rows, cols = vol_ref.shape
    body_rows = TV_STEPS * rows
    part = STRIDE * TV_STEPS
    depth = slab + 2 * TV_STEPS
    base = 16
    lane3 = lax.broadcasted_iota(jnp.int32, (TV_STEPS, cols), 1)
    first, last = lane_masks()
    turn[...] = jnp.zeros_like(turn)
    for z in range(depth):
        s = z - TV_STEPS
        if 0 <= s < slab:
            tile = vol_ref[s]
            near = [near_ref[i, pl.ds(STRIDE * s, TV_STEPS), :] for i in range(8)]
        else:
            src, k = (low_ref, z) if s < 0 else (high_ref, s - slab)
            tile = src[pl.ds(rows * k, rows), :]
            near = [src[pl.ds(body_rows + part * i + STRIDE * k, TV_STEPS), :] for i in range(8)]
        for half in range(2):
            v[z, half, pl.ds(0, base), :] = jnp.zeros((base, cols), jnp.float32)
            v[z, half, pl.ds(base + rows, 16), :] = jnp.zeros((16, cols), jnp.float32)
        v[z, 0, pl.ds(base, rows), :] = tile
        v[z, 0, pl.ds(base - TV_STEPS, TV_STEPS), :] = near[0]
        v[z, 0, pl.ds(base + rows, TV_STEPS), :] = near[1]
        for row, k in ((0, 2), (cols - TV_STEPS, 5)):
            above, beside, below = near[k : k + 3]
            ends = jnp.where(lane3 < 3 * cols // 4, pltpu.roll(below, rows, 1), pltpu.roll(above, rows, 1))
            turn[pl.ds(row, TV_STEPS), :] = jnp.where(lane3 < rows, beside, ends)
        sides = turn[...].T
        v[z, 1, pl.ds(base, rows), :] = sides[:rows]
        v[z, 1, pl.ds(base + rows, TV_STEPS), :] = sides[rows : rows + TV_STEPS]
        v[z, 1, pl.ds(base - TV_STEPS, TV_STEPS), :] = sides[cols - TV_STEPS :]

    z_first = lax.axis_index("angle") * slab - TV_STEPS + nz
    chunks = rows // 8 + 2
    for t in range(TV_STEPS):

        @pl.loop(t, depth - 1 - t)
        def _(z):
            inner = jnp.where(lax.rem(z_first + z, nz) == nz - 1, 0.0, 1.0)
            for c in range(chunks):
                row = base - 8 + 8 * c
                mid = [v[z, half, pl.ds(row, 8), :] for half in range(2)]
                ahead = [pltpu.roll(m, cols - 1, 1) for m in mid]
                for half in range(2):
                    dz = (v[z + 1, half, pl.ds(row, 8), :] - mid[half]) * inner
                    dy = v[z, half, pl.ds(row + 1, 8), :] - mid[half]
                    dx = jnp.where(last, ahead[1 - half], ahead[half]) - mid[half]
                    scale = lax.rsqrt(dz * dz + dy * dy + dx * dx + tv_smooth * tv_smooth)
                    fz[z, half, pl.ds(row, 8), :] = dz * scale
                    fy[z, half, pl.ds(row, 8), :] = dy * scale
                    fx[z, half, pl.ds(row, 8), :] = dx * scale

        @pl.loop(t + 1, depth - 1 - t)
        def _(z):
            final = t == TV_STEPS - 1
            for c in range(1, chunks - 1) if final else range(chunks):
                row = base - 8 + 8 * c
                mid = [fx[z, half, pl.ds(row, 8), :] for half in range(2)]
                behind = [pltpu.roll(m, 1, 1) for m in mid]
                for half in range(1 if final else 2):
                    here = pl.ds(row, 8)
                    div = fz[z, half, here, :] - fz[z - 1, half, here, :]
                    div = div + (fy[z, half, here, :] - fy[z, half, pl.ds(row - 1, 8), :])
                    div = div + (mid[half] - jnp.where(first, behind[1 - half], behind[half]))
                    new = v[z, half, here, :] + tv_rate * div
                    if final:
                        out_ref[z - TV_STEPS, pl.ds(row - base, 8), :] = new
                    else:
                        v[z, half, here, :] = new


def step_and_smooth(parts, index, nz):
    slab, rows, cols = index.shape
    nx, ny = lax.axis_size("tx"), lax.axis_size("ty")
    block = jax.ShapeDtypeStruct(index.shape, jnp.float32)
    params = pltpu.CompilerParams(vmem_limit_bytes=40 * 2**20)
    strip_rows = STRIDE * slab
    gradient, volume, strips = pl.pallas_call(
        functools.partial(share_kernel, nx, ny),
        out_shape=(block, block, jax.ShapeDtypeStruct((nx * ny, strip_rows, cols), jnp.float32)),
        compiler_params=params,
        name="share",
    )(parts, index)
    strips = lax.all_to_all(strips, ("tx", "ty"), 0, 0, tiled=True)
    outward = jax.ShapeDtypeStruct((TV_STEPS * (rows + 8 * STRIDE), cols), jnp.float32)
    near, up, down = pl.pallas_call(
        functools.partial(sort_kernel, nx, ny),
        out_shape=(jax.ShapeDtypeStruct((8, strip_rows, cols), jnp.float32), outward, outward),
        compiler_params=params,
        name="sort",
    )(strips, volume)
    depth = lax.axis_size("angle")
    low = lax.ppermute(up, "angle", ring(depth, 1))
    high = lax.ppermute(down, "angle", ring(depth, -1))
    whole = pltpu.VMEM((slab + 2 * TV_STEPS, 2, rows + 32, cols), jnp.float32)
    smoothed = pl.pallas_call(
        functools.partial(smooth_kernel, nz),
        out_shape=block,
        scratch_shapes=[whole, whole, whole, whole, pltpu.VMEM((cols, cols), jnp.float32)],
        compiler_params=params,
        name="smooth",
    )(volume, near, low, high)
    return gradient, smoothed


def body(index, measured, illum):
    slab, rows, cols = index.shape
    depth = lax.axis_size("angle")
    nz = slab * depth
    nx = cols * lax.axis_size("tx")
    ny = rows * lax.axis_size("ty")
    tall = 3 * rows
    core_groups = [[2 * i, 2 * i + 1] for i in range(depth // 2)]
    chip_groups = [list(range(c, depth, 2)) for c in range(2)]

    half = lax.broadcasted_iota(jnp.int32, (2, tall, cols), 0)
    lane = lax.broadcasted_iota(jnp.int32, (2, tall, cols), 2)
    gx = lax.axis_index("tx") * cols + jnp.where(half == 0, lane, jnp.where(lane < cols // 2, lane + cols, lane - cols))
    gy = lax.axis_index("ty") * rows - rows + lax.broadcasted_iota(jnp.int32, (2, tall, cols), 1)
    turns = (illum[0, 0] * gx * (ny // math.gcd(nx, ny)) + illum[0, 1] * gy * (nx // math.gcd(nx, ny)))
    whole = math.lcm(nx, ny)
    turns = lax.rem(lax.rem(turns, whole) + whole, whole)
    q = (2.0 * math.pi / whole) * turns.astype(jnp.float32)
    start = jnp.stack([jnp.cos(q), jnp.sin(q)])

    column = lax.all_gather(pack_corners(*widen(index, "tx", "ty")), "angle", axis=0, tiled=True)

    index_block = (GROUP, 5 * rows, cols)
    field_block = (GROUP, 2, rows, cols)
    steps = nz // GROUP
    scratch = [pltpu.VMEM((2, 4, tall + 16, cols), jnp.float32)]
    params = pltpu.CompilerParams(dimension_semantics=("arbitrary",), vmem_limit_bytes=40 * 2**20)
    fields = pl.pallas_call(
        functools.partial(forward_kernel, tall),
        grid=(steps,),
        in_specs=[
            pl.BlockSpec(index_block, lambda i: (i, 0, 0)),
            pl.BlockSpec((2, 2, tall, cols), lambda i: (0, 0, 0, 0)),
        ],
        out_specs=pl.BlockSpec(field_block, lambda i: (i, 0, 0, 0)),
        out_shape=jax.ShapeDtypeStruct((nz, 2, rows, cols), jnp.float32),
        scratch_shapes=scratch,
        compiler_params=params,
        name="forward",
    )(column, start)

    back = (TURN.conjugate() ** nz)
    back = back / abs(back)
    target_re = back.real * measured[0] - back.imag * measured[1]
    target_im = back.real * measured[1] + back.imag * measured[0]
    residual = fields[nz - 1] - jnp.concatenate([target_re, target_im], axis=0)
    adjoint = jnp.concatenate(widen(residual, "tx", "ty"), axis=2)

    grads = pl.pallas_call(
        functools.partial(backward_kernel, tall),
        grid=(steps,),
        in_specs=[
            pl.BlockSpec(index_block, lambda i: (steps - 1 - i, 0, 0)),
            pl.BlockSpec((2, 2, tall, cols), lambda i: (0, 0, 0, 0)),
            pl.BlockSpec(field_block, lambda i: (steps - 1 - i, 0, 0, 0)),
        ],
        out_specs=pl.BlockSpec((2, 1, slab, rows, cols), lambda i: (0, steps - 1 - i, 0, 0, 0)),
        out_shape=jax.ShapeDtypeStruct((2, depth // 2, slab, rows, cols), jnp.float32),
        scratch_shapes=scratch,
        compiler_params=params,
        name="backward",
    )(column, adjoint, fields)

    pair = lax.all_to_all(grads, "angle", 0, 0, tiled=True, axis_index_groups=core_groups)
    both = pair[0] + pair[1]
    parts = lax.all_to_all(both, "angle", 0, 0, tiled=True, axis_index_groups=chip_groups)
    return step_and_smooth(parts, index, nz)


def solution(mesh):
    in_specs = (P("angle", "ty", "tx"), P(None, "angle", "ty", "tx"), P("angle", None))
    out_specs = (P("angle", "ty", "tx"), P("angle", "ty", "tx"))
    return jax.shard_map(body, mesh=mesh, in_specs=in_specs, out_specs=out_specs, check_vma=False)
```

```python
import functools
import math

import jax
import jax.numpy as jnp
import numpy as np
from jax import lax
from jax.experimental import pallas as pl
from jax.experimental.pallas import tpu as pltpu
from jax.sharding import PartitionSpec as P

TV_STEPS = 3
GROUP = 8

damping = 0.2
disperse = 0.1
phase_scale = 0.1
step_size = 0.1
tv_rate = 0.05
tv_smooth = 0.1

SPREAD = complex(damping, disperse)
GAIN = abs(SPREAD)
TURN = SPREAD / GAIN


def _fit():
    nodes = np.cos((np.arange(400) + 0.5) * np.pi / 400)
    t = 3.05 * (nodes + 1.0)
    z = t * t
    scaled = z / z.max()
    even = np.linalg.lstsq(scaled[:, None] ** np.arange(4), GAIN * np.cos(phase_scale * t), rcond=None)[0]
    odd = np.linalg.lstsq(scaled[:, None] ** np.arange(4), GAIN * np.sin(phase_scale * t) / t, rcond=None)[0]
    powers = z.max() ** np.arange(4)
    return [float(v) for v in even / powers], [float(v) for v in odd / powers]


EVEN, ODD = _fit()


def phase_factor(t):
    z = t * t
    cosine = EVEN[3]
    for coef in EVEN[2::-1]:
        cosine = cosine * z + coef
    sine = ODD[3]
    for coef in ODD[2::-1]:
        sine = sine * z + coef
    return cosine, sine * t


def neighbours(buf, slot, part, row, first, last):
    mid = [buf[slot, 2 * part + half, pl.ds(row, 8), :] for half in range(2)]
    low = [pltpu.roll(m, 1, 1) for m in mid]
    high = [pltpu.roll(m, 127, 1) for m in mid]
    out = []
    for half in range(2):
        left = jnp.where(first, low[1 - half], low[half])
        right = jnp.where(last, high[1 - half], high[half])
        up = buf[slot, 2 * part + half, pl.ds(row - 1, 8), :]
        down = buf[slot, 2 * part + half, pl.ds(row + 1, 8), :]
        out.append((left + right) + (up + down))
    return mid, out


def lane_masks():
    lane = lax.broadcasted_iota(jnp.int32, (8, 128), 1)
    return lane == 0, lane == 127


def near_lanes():
    lane = lax.broadcasted_iota(jnp.int32, (8, 128), 1)
    return (lane < 32) | (lane >= 96)


def near_index(near_ref, pair, odd, half, c):
    tall = near_ref.shape[1] // 3
    if half == 0:
        return near_ref[pair, pl.ds(tall * odd + 8 * c, 8), :]
    rows = near_ref[pair, pl.ds(2 * tall + 8 * c, 8), :]
    return pltpu.roll(rows, 64, 1) if odd else rows


def full_index(near_ref, far_ref, pair, odd, half, c, is_near):
    tall = near_ref.shape[1] // 3
    edge = tall // 4
    rim = edge // 8
    cn = c - rim
    corner = 4 * edge + tall + edge * odd
    if 0 <= cn < tall // 8:
        if half == 0:
            return near_index(near_ref, pair, odd, half, cn)
        inner = near_ref[pair, pl.ds(2 * tall + 8 * cn, 8), :]
        outer = far_ref[pair, pl.ds(4 * edge + 8 * cn, 8), :]
        if odd:
            return pltpu.roll(jnp.where(is_near, outer, inner), 64, 1)
        return jnp.where(is_near, inner, outer)
    if cn < 0:
        if half == 0:
            return far_ref[pair, pl.ds(2 * edge * odd + 8 * c, 8), :]
        return far_ref[pair, pl.ds(corner + 8 * c, 8), :]
    c = cn - tall // 8
    if half == 0:
        return far_ref[pair, pl.ds(2 * edge * odd + edge + 8 * c, 8), :]
    return pltpu.roll(far_ref[pair, pl.ds(corner + 8 * c, 8), :], 64, 1)


def forward_kernel(near_ref, start_ref, field_ref, buf):
    tall = start_ref.shape[2]
    chunks = tall // 8
    own_first = (tall - field_ref.shape[2]) // 16
    own_last = chunks - own_first
    pid = pl.program_id(0)
    first, last = lane_masks()

    @pl.when(pid == 0)
    def _():
        buf[...] = jnp.zeros_like(buf)
        for q in range(4):
            buf[0, q, 8 : 8 + tall, :] = start_ref[q // 2, q % 2]

    def step(pair, odd, lo, hi):
        for c in range(lo, hi):
            row = 8 + 8 * c
            re, sum_re = neighbours(buf, odd, 0, row, first, last)
            im, sum_im = neighbours(buf, odd, 1, row, first, last)
            for half in range(2):
                cosine, sine = phase_factor(near_index(near_ref, pair, odd, half, c))
                wre = sum_re[half] + (im[half] + im[half])
                wim = sum_im[half] - (re[half] + re[half])
                nre = cosine * wre - sine * wim
                nim = cosine * wim + sine * wre
                buf[1 - odd, half, pl.ds(row, 8), :] = nre
                buf[1 - odd, 2 + half, pl.ds(row, 8), :] = nim
                if half == 0 and own_first <= c < own_last:
                    own = pl.ds(8 * (c - own_first), 8)
                    field_ref[2 * pair + odd, 0, own, :] = nre
                    field_ref[2 * pair + odd, 1, own, :] = nim

    for k in range(own_first):

        @pl.when(pid == k)
        def _(k=k):
            @pl.loop(0, GROUP // 2)
            def _(pair):
                step(pair, 0, k, chunks - k)
                step(pair, 1, k, chunks - k)


def backward_kernel(near_ref, far_ref, start_ref, early_ref, late_ref, grad_ref, buf):
    tall = start_ref.shape[2]
    chunks = tall // 8
    own_first = (tall - early_ref.shape[2]) // 16
    own_last = chunks - own_first
    rim = own_first // 2
    pid = pl.program_id(0)
    first, last = lane_masks()
    is_near = near_lanes()
    slab = GROUP // 2

    @pl.when(pid == 0)
    def _():
        buf[...] = jnp.zeros_like(buf)

    def finish(wide, pair, odd, c, half, are, aim):
        j = 2 * pair + odd
        if half == 0 and own_first <= c < own_last:
            own = pl.ds(8 * (c - own_first), 8)
            field_ref = late_ref if wide else early_ref
            fre = field_ref[j, 0, own, :]
            fim = field_ref[j, 1, own, :]
            grad_ref[j // slab, 0, j % slab, own, :] = phase_scale * (aim * fre - are * fim)
        if wide:
            index = full_index(near_ref, far_ref, pair, odd, half, c, is_near)
        else:
            index = near_index(near_ref, pair, odd, half, c - rim)
        cosine, sine = phase_factor(index)
        row = pl.ds(8 + 8 * c, 8)
        buf[odd, half, row, :] = cosine * are + sine * aim
        buf[odd, 2 + half, row, :] = cosine * aim - sine * are

    def step(wide, pair, odd, lo, hi):
        for c in range(lo, hi):
            row = 8 + 8 * c
            re, sum_re = neighbours(buf, 1 - odd, 0, row, first, last)
            im, sum_im = neighbours(buf, 1 - odd, 1, row, first, last)
            for half in range(2):
                are = sum_re[half] - (im[half] + im[half])
                aim = sum_im[half] + (re[half] + re[half])
                finish(wide, pair, odd, c, half, are, aim)

    for k in range(own_first):

        @pl.when(pid == k)
        def _(k=k):
            wide = k < rim
            top = GROUP // 2 - 1
            if k == 0:
                for c in range(chunks):
                    for half in range(2):
                        rows = pl.ds(8 * c, 8)
                        finish(wide, top, 1, c, half, start_ref[0, half, rows, :], start_ref[1, half, rows, :])
                step(wide, top, 0, k, chunks - k)

            @pl.loop(1 if k == 0 else 0, GROUP // 2)
            def _(back):
                step(wide, top - back, 1, k, chunks - k)
                step(wide, top - back, 0, k, chunks - k)


def ring(count, by):
    return [(i, (i + by) % count) for i in range(count)]


def widen_x(block):
    n, rows, cols = block.shape
    half = cols // 2
    nx = lax.axis_size("tx")
    pack = lambda v: jnp.concatenate([v[: n // 2], v[n // 2 :]], axis=2)
    unpack = lambda v: jnp.concatenate([v[:, :, :half], v[:, :, half:]], axis=0)
    left = unpack(lax.ppermute(pack(block[:, :, half:]), "tx", ring(nx, 1)))
    right = unpack(lax.ppermute(pack(block[:, :, :half]), "tx", ring(nx, -1)))
    return jnp.stack([block, jnp.concatenate([right, left], axis=2)], axis=1)


def rows_around(wide, start, stop):
    rows = wide.shape[2]
    ny = lax.axis_size("ty")
    above = lax.ppermute(wide[:, :, rows - stop : rows - start], "ty", ring(ny, 1))
    below = lax.ppermute(wide[:, :, start:stop], "ty", ring(ny, -1))
    return above, below


def widen(block, reach):
    wide = widen_x(block)
    above, below = rows_around(wide, 0, reach)
    return jnp.concatenate([above, wide, below], axis=2)


def turned(block):
    return jnp.roll(block, block.shape[-1] // 2, axis=-1)


def gather_index(index):
    slab, rows, cols = index.shape
    reach = rows // 2
    lane = lax.broadcasted_iota(jnp.int32, (1, cols), 1)
    inner = (lane < cols // 4) | (lane >= cols - cols // 4)
    wide = widen_x(index)
    above, below = rows_around(wide, 0, reach)
    tall = rows + 2 * reach
    sides = jnp.concatenate([above[:, 1], wide[:, 1], below[:, 1]], axis=1).reshape(slab // 2, 2, tall, cols)
    even, odd = sides[:, 0], turned(sides[:, 1])
    middle = jnp.concatenate([above[:, 0], wide[:, 0], below[:, 0]], axis=1).reshape(slab // 2, 2 * tall, cols)
    near = jnp.concatenate([middle, jnp.where(inner, even, odd)], axis=1)
    near = lax.all_gather(near, "angle", axis=0, tiled=True)
    above, below = rows_around(wide, reach, 2 * reach)
    middle = jnp.concatenate([above[:, 0], below[:, 0]], axis=1).reshape(slab // 2, 4 * reach, cols)
    corners = jnp.where(inner, above[:, 1], turned(below[:, 1])).reshape(slab // 2, 2 * reach, cols)
    far = jnp.concatenate([middle, jnp.where(inner, odd, even), corners], axis=1)
    far = lax.all_gather(far, "angle", axis=0, tiled=True)
    return near, far


AROUND = [(0, -1), (0, 1), (1, -1), (1, 0), (1, 1), (-1, -1), (-1, 0), (-1, 1)]
STRIDE = 4


def tile_at(nx, ny, dx, dy):
    tx, ty = lax.axis_index("tx"), lax.axis_index("ty")
    return lax.rem(tx + dx + nx, nx) * ny + lax.rem(ty + dy + ny, ny)


def share_kernel(nx, ny, parts_ref, index_ref, grad_ref, vol_ref, out_ref):
    slab, rows, cols = index_ref.shape
    out_ref[...] = jnp.zeros_like(out_ref)
    for s in range(slab):
        grad = parts_ref[0, s]
        for p in range(1, parts_ref.shape[0]):
            grad = grad + parts_ref[p, s]
        vol = index_ref[s] - step_size * grad
        grad_ref[s] = grad
        vol_ref[s] = vol
        turned = vol.T
        keep = pl.ds(STRIDE * s, TV_STEPS)
        for dx, dy in AROUND:
            spot = tile_at(nx, ny, dx, dy)
            if dx == 0:
                out_ref[spot, keep, :] = vol[rows - TV_STEPS :] if dy > 0 else vol[:TV_STEPS]
            else:
                out_ref[spot, keep, :rows] = turned[cols - TV_STEPS :] if dx > 0 else turned[:TV_STEPS]


def sort_kernel(nx, ny, strips_ref, vol_ref, near_ref, up_ref, down_ref):
    slab, rows, cols = vol_ref.shape
    body_rows = TV_STEPS * rows
    part = STRIDE * TV_STEPS
    for s in range(TV_STEPS):
        down_ref[pl.ds(rows * s, rows), :] = vol_ref[s]
        up_ref[pl.ds(rows * s, rows), :] = vol_ref[slab - TV_STEPS + s]
    for i, (dx, dy) in enumerate(AROUND):
        strip = strips_ref[tile_at(nx, ny, dx, dy)]
        near_ref[i] = strip
        down_ref[pl.ds(body_rows + part * i, part), :] = strip[:part]
        up_ref[pl.ds(body_rows + part * i, part), :] = strip[STRIDE * (slab - TV_STEPS) :]


def smooth_kernel(nz, vol_ref, near_ref, low_ref, high_ref, out_ref, v, fz, fy, fx, turn):
    slab, rows, cols = vol_ref.shape
    body_rows = TV_STEPS * rows
    part = STRIDE * TV_STEPS
    depth = slab + 2 * TV_STEPS
    base = 16
    lane3 = lax.broadcasted_iota(jnp.int32, (TV_STEPS, cols), 1)
    first, last = lane_masks()
    turn[...] = jnp.zeros_like(turn)
    for z in range(depth):
        s = z - TV_STEPS
        if 0 <= s < slab:
            tile = vol_ref[s]
            near = [near_ref[i, pl.ds(STRIDE * s, TV_STEPS), :] for i in range(8)]
        else:
            src, k = (low_ref, z) if s < 0 else (high_ref, s - slab)
            tile = src[pl.ds(rows * k, rows), :]
            near = [src[pl.ds(body_rows + part * i + STRIDE * k, TV_STEPS), :] for i in range(8)]
        for half in range(2):
            v[z, half, pl.ds(0, base), :] = jnp.zeros((base, cols), jnp.float32)
            v[z, half, pl.ds(base + rows, 16), :] = jnp.zeros((16, cols), jnp.float32)
        v[z, 0, pl.ds(base, rows), :] = tile
        v[z, 0, pl.ds(base - TV_STEPS, TV_STEPS), :] = near[0]
        v[z, 0, pl.ds(base + rows, TV_STEPS), :] = near[1]
        for row, k in ((0, 2), (cols - TV_STEPS, 5)):
            above, beside, below = near[k : k + 3]
            ends = jnp.where(lane3 < 3 * cols // 4, pltpu.roll(below, rows, 1), pltpu.roll(above, rows, 1))
            turn[pl.ds(row, TV_STEPS), :] = jnp.where(lane3 < rows, beside, ends)
        sides = turn[...].T
        v[z, 1, pl.ds(base, rows), :] = sides[:rows]
        v[z, 1, pl.ds(base + rows, TV_STEPS), :] = sides[rows : rows + TV_STEPS]
        v[z, 1, pl.ds(base - TV_STEPS, TV_STEPS), :] = sides[cols - TV_STEPS :]

    z_first = lax.axis_index("angle") * slab - TV_STEPS + nz
    chunks = rows // 8 + 2
    for t in range(TV_STEPS):

        @pl.loop(t, depth - 1 - t)
        def _(z):
            inner = jnp.where(lax.rem(z_first + z, nz) == nz - 1, 0.0, 1.0)
            for c in range(chunks):
                row = base - 8 + 8 * c
                mid = [v[z, half, pl.ds(row, 8), :] for half in range(2)]
                ahead = [pltpu.roll(m, cols - 1, 1) for m in mid]
                for half in range(2):
                    dz = (v[z + 1, half, pl.ds(row, 8), :] - mid[half]) * inner
                    dy = v[z, half, pl.ds(row + 1, 8), :] - mid[half]
                    dx = jnp.where(last, ahead[1 - half], ahead[half]) - mid[half]
                    scale = lax.rsqrt(dz * dz + dy * dy + dx * dx + tv_smooth * tv_smooth)
                    fz[z, half, pl.ds(row, 8), :] = dz * scale
                    fy[z, half, pl.ds(row, 8), :] = dy * scale
                    fx[z, half, pl.ds(row, 8), :] = dx * scale

        @pl.loop(t + 1, depth - 1 - t)
        def _(z):
            final = t == TV_STEPS - 1
            for c in range(1, chunks - 1) if final else range(chunks):
                row = base - 8 + 8 * c
                mid = [fx[z, half, pl.ds(row, 8), :] for half in range(2)]
                behind = [pltpu.roll(m, 1, 1) for m in mid]
                for half in range(1 if final else 2):
                    here = pl.ds(row, 8)
                    div = fz[z, half, here, :] - fz[z - 1, half, here, :]
                    div = div + (fy[z, half, here, :] - fy[z, half, pl.ds(row - 1, 8), :])
                    div = div + (mid[half] - jnp.where(first, behind[1 - half], behind[half]))
                    new = v[z, half, here, :] + tv_rate * div
                    if final:
                        out_ref[z - TV_STEPS, pl.ds(row - base, 8), :] = new
                    else:
                        v[z, half, here, :] = new


def step_and_smooth(parts, index, nz):
    slab, rows, cols = index.shape
    nx, ny = lax.axis_size("tx"), lax.axis_size("ty")
    block = jax.ShapeDtypeStruct(index.shape, jnp.float32)
    params = pltpu.CompilerParams(vmem_limit_bytes=40 * 2**20)
    strip_rows = STRIDE * slab
    gradient, volume, strips = pl.pallas_call(
        functools.partial(share_kernel, nx, ny),
        out_shape=(block, block, jax.ShapeDtypeStruct((nx * ny, strip_rows, cols), jnp.float32)),
        compiler_params=params,
        name="share",
    )(parts, index)
    strips = lax.all_to_all(strips, ("tx", "ty"), 0, 0, tiled=True)
    outward = jax.ShapeDtypeStruct((TV_STEPS * (rows + 8 * STRIDE), cols), jnp.float32)
    near, up, down = pl.pallas_call(
        functools.partial(sort_kernel, nx, ny),
        out_shape=(jax.ShapeDtypeStruct((8, strip_rows, cols), jnp.float32), outward, outward),
        compiler_params=params,
        name="sort",
    )(strips, volume)
    depth = lax.axis_size("angle")
    low = lax.ppermute(up, "angle", ring(depth, 1))
    high = lax.ppermute(down, "angle", ring(depth, -1))
    whole = pltpu.VMEM((slab + 2 * TV_STEPS, 2, rows + 32, cols), jnp.float32)
    smoothed = pl.pallas_call(
        functools.partial(smooth_kernel, nz),
        out_shape=block,
        scratch_shapes=[whole, whole, whole, whole, pltpu.VMEM((cols, cols), jnp.float32)],
        compiler_params=params,
        name="smooth",
    )(volume, near, low, high)
    return gradient, smoothed


def incident(illum, shape, reach):
    rows, cols = shape
    nx = cols * lax.axis_size("tx")
    ny = rows * lax.axis_size("ty")
    block = (2, rows + 2 * reach, cols)
    half = lax.broadcasted_iota(jnp.int32, block, 0)
    lane = lax.broadcasted_iota(jnp.int32, block, 2)
    beside = jnp.where(lane < cols // 2, lane + cols, lane - cols)
    gx = lax.axis_index("tx") * cols + jnp.where(half == 0, lane, beside)
    gy = lax.axis_index("ty") * rows - reach + lax.broadcasted_iota(jnp.int32, block, 1)
    whole = math.lcm(nx, ny)
    parts = illum[0, 0] * gx * (whole // nx) + illum[0, 1] * gy * (whole // ny)
    parts = lax.rem(lax.rem(parts, whole) + whole, whole)
    q = (2.0 * math.pi / whole) * parts.astype(jnp.float32)
    return jnp.stack([jnp.cos(q), jnp.sin(q)])


def body(index, measured, illum):
    slab, rows, cols = index.shape
    depth = lax.axis_size("angle")
    nz = slab * depth
    reach = rows // 2
    core_groups = [[2 * i, 2 * i + 1] for i in range(depth // 2)]
    chip_groups = [list(range(c, depth, 2)) for c in range(2)]

    near, far = gather_index(index)

    steps = nz // GROUP
    near_block = (GROUP // 2,) + near.shape[1:]
    far_block = (GROUP // 2,) + far.shape[1:]
    field_block = (GROUP, 2, rows, cols)
    params = pltpu.CompilerParams(dimension_semantics=("arbitrary",), vmem_limit_bytes=40 * 2**20)

    def forward(start, first_step):
        whole = pl.BlockSpec(start.shape, lambda i: (0, 0, 0, 0))
        return pl.pallas_call(
            forward_kernel,
            grid=(steps // 2,),
            in_specs=[pl.BlockSpec(near_block, lambda i: (i + first_step, 0, 0)), whole],
            out_specs=pl.BlockSpec(field_block, lambda i: (i, 0, 0, 0)),
            out_shape=jax.ShapeDtypeStruct((nz // 2, 2, rows, cols), jnp.float32),
            scratch_shapes=[pltpu.VMEM((2, 4, rows + 2 * reach + 16, cols), jnp.float32)],
            compiler_params=params,
            name="forward",
        )(near, start)

    early = forward(incident(illum, (rows, cols), reach), 0)
    late = forward(widen(early[nz // 2 - 1], reach), steps // 2)

    back = TURN.conjugate() ** nz
    back = back / abs(back)
    target_re = back.real * measured[0] - back.imag * measured[1]
    target_im = back.real * measured[1] + back.imag * measured[0]
    residual = late[nz // 2 - 1] - jnp.concatenate([target_re, target_im], axis=0)
    adjoint = widen(residual, rows)

    grads = pl.pallas_call(
        backward_kernel,
        grid=(steps,),
        in_specs=[
            pl.BlockSpec(near_block, lambda i: (steps - 1 - i, 0, 0)),
            pl.BlockSpec(far_block, lambda i: (jnp.maximum(steps - 1 - i, steps // 2), 0, 0)),
            pl.BlockSpec(adjoint.shape, lambda i: (0, 0, 0, 0)),
            pl.BlockSpec(field_block, lambda i: (jnp.minimum(steps - 1 - i, steps // 2 - 1), 0, 0, 0)),
            pl.BlockSpec(field_block, lambda i: (jnp.maximum(steps // 2 - 1 - i, 0), 0, 0, 0)),
        ],
        out_specs=pl.BlockSpec((2, 1, slab, rows, cols), lambda i: (0, steps - 1 - i, 0, 0, 0)),
        out_shape=jax.ShapeDtypeStruct((2, depth // 2, slab, rows, cols), jnp.float32),
        scratch_shapes=[pltpu.VMEM((2, 4, 3 * rows + 16, cols), jnp.float32)],
        compiler_params=params,
        name="backward",
    )(near, far, adjoint, early, late)

    pair = lax.all_to_all(grads, "angle", 0, 0, tiled=True, axis_index_groups=core_groups)
    both = pair[0] + pair[1]
    parts = lax.all_to_all(both, "angle", 0, 0, tiled=True, axis_index_groups=chip_groups)
    return step_and_smooth(parts, index, nz)


def solution(mesh):
    in_specs = (P("angle", "ty", "tx"), P(None, "angle", "ty", "tx"), P("angle", None))
    out_specs = (P("angle", "ty", "tx"), P("angle", "ty", "tx"))
    return jax.shard_map(body, mesh=mesh, in_specs=in_specs, out_specs=out_specs, check_vma=False)
```

```python
import functools
import math

import jax
import jax.numpy as jnp
import numpy as np
from jax import lax
from jax.experimental import pallas as pl
from jax.experimental.pallas import tpu as pltpu
from jax.sharding import PartitionSpec as P

TV_STEPS = 3
HALO = 64
GROUP = 8

damping = 0.2
disperse = 0.1
phase_scale = 0.1
step_size = 0.1
tv_rate = 0.05
tv_smooth = 0.1

SPREAD = complex(damping, disperse)
GAIN = abs(SPREAD)
TURN = SPREAD / GAIN


def _fit():
    nodes = np.cos((np.arange(400) + 0.5) * np.pi / 400)
    t = 3.05 * (nodes + 1.0)
    z = t * t
    scaled = z / z.max()
    even = np.linalg.lstsq(scaled[:, None] ** np.arange(4), GAIN * np.cos(phase_scale * t), rcond=None)[0]
    odd = np.linalg.lstsq(scaled[:, None] ** np.arange(4), GAIN * np.sin(phase_scale * t) / t, rcond=None)[0]
    powers = z.max() ** np.arange(4)
    return [float(v) for v in even / powers], [float(v) for v in odd / powers]


EVEN, ODD = _fit()


def phase_factor(t):
    z = t * t
    cosine = EVEN[3]
    for coef in EVEN[2::-1]:
        cosine = cosine * z + coef
    sine = ODD[3]
    for coef in ODD[2::-1]:
        sine = sine * z + coef
    return cosine, sine * t


def neighbours(buf, slot, part, row):
    even, odd = [buf[slot, 2 * part + parity, pl.ds(row, 8), :] for parity in range(2)]
    sides = (odd + pltpu.roll(odd, 1, 1), even + pltpu.roll(even, 127, 1))
    out = []
    for parity in range(2):
        up = buf[slot, 2 * part + parity, pl.ds(row - 1, 8), :]
        down = buf[slot, 2 * part + parity, pl.ds(row + 1, 8), :]
        out.append(sides[parity] + (up + down))
    return (even, odd), out


def index_rows(index_ref, j, parity, c, chunks):
    third = chunks // 3
    rows = index_ref.shape[1] // 5
    if c < 2 * third:
        return index_ref[j, pl.ds(2 * rows * parity + 8 * c, 8), :]
    c = c - 2 * third
    corner = index_ref[j, pl.ds(2 * rows * parity + 8 * c, 8), :]
    own = index_ref[j, pl.ds(4 * rows + 8 * c, 8), :]
    if parity:
        own = pltpu.roll(own, 64, 1)
    lane = lax.broadcasted_iota(jnp.int32, (8, 128), 1)
    corner = jnp.where(lane < 96, pltpu.roll(corner, 96, 1), pltpu.roll(corner, 32, 1))
    return jnp.where(lane < 64, own, corner)


def lane_masks():
    lane = lax.broadcasted_iota(jnp.int32, (8, 128), 1)
    return lane == 0, lane == 127


def forward_kernel(rows, index_ref, start_ref, field_ref, buf):
    chunks = rows // 8
    pid = pl.program_id(0)

    @pl.when(pid == 0)
    def _():
        buf[...] = jnp.zeros_like(buf)
        for q in range(4):
            buf[0, q, 8 : 8 + rows, :] = start_ref[q // 2, q % 2]

    def step(j, parity, lo, hi):
        for c in range(lo, hi):
            row = 8 + 8 * c
            re, sum_re = neighbours(buf, parity, 0, row)
            im, sum_im = neighbours(buf, parity, 1, row)
            for half in range(2):
                cosine, sine = phase_factor(index_rows(index_ref, j, half, c, chunks))
                wre = sum_re[half] + (im[half] + im[half])
                wim = sum_im[half] - (re[half] + re[half])
                nre = cosine * wre - sine * wim
                nim = cosine * wim + sine * wre
                buf[1 - parity, half, pl.ds(row, 8), :] = nre
                buf[1 - parity, 2 + half, pl.ds(row, 8), :] = nim
                if chunks // 3 <= c < 2 * chunks // 3:
                    own = 8 * (c - chunks // 3)
                    field_ref[j, 0, half, pl.ds(own, 8), :] = nre
                    field_ref[j, 1, half, pl.ds(own, 8), :] = nim

    for k in range(8):

        @pl.when(pid == k)
        def _(k=k):
            @pl.loop(0, GROUP // 2)
            def _(pair):
                step(2 * pair, 0, k, chunks - k)
                step(2 * pair + 1, 1, k, chunks - k)


def backward_kernel(rows, index_ref, start_ref, field_ref, grad_ref, buf):
    chunks = rows // 8
    pid = pl.program_id(0)

    @pl.when(pid == 0)
    def _():
        buf[...] = jnp.zeros_like(buf)

    def finish(j, slot, c, are, aim):
        if chunks // 3 <= c < 2 * chunks // 3:
            own = pl.ds(8 * (c - chunks // 3), 8)
            parts = []
            for half in range(2):
                fre = field_ref[j, 0, half, own, :]
                fim = field_ref[j, 1, half, own, :]
                parts.append(phase_scale * (aim[half] * fre - are[half] * fim))
            slab = GROUP // 2
            lane = lax.broadcasted_iota(jnp.int32, (8, 128), 1)
            both = jnp.where(lane < 64, parts[0], pltpu.roll(parts[1], 64, 1))
            grad_ref[j // slab, 0, j % slab, own, :] = both
        row = 8 + 8 * c
        for half in range(2):
            cosine, sine = phase_factor(index_rows(index_ref, j, half, c, chunks))
            buf[slot, half, pl.ds(row, 8), :] = cosine * are[half] + sine * aim[half]
            buf[slot, 2 + half, pl.ds(row, 8), :] = cosine * aim[half] - sine * are[half]

    def step(j, parity, lo, hi):
        for c in range(lo, hi):
            row = 8 + 8 * c
            re, sum_re = neighbours(buf, 1 - parity, 0, row)
            im, sum_im = neighbours(buf, 1 - parity, 1, row)
            are = [sum_re[half] - (im[half] + im[half]) for half in range(2)]
            aim = [sum_im[half] + (re[half] + re[half]) for half in range(2)]
            finish(j, parity, c, are, aim)

    for k in range(8):

        @pl.when(pid == k)
        def _(k=k):
            skip = 0
            if k == 0:
                skip = 1
                for c in range(chunks):
                    here = pl.ds(8 * c, 8)
                    finish(
                        GROUP - 1,
                        1,
                        c,
                        [start_ref[0, half, here, :] for half in range(2)],
                        [start_ref[1, half, here, :] for half in range(2)],
                    )
                step(GROUP - 2, 0, k, chunks - k)

            @pl.loop(skip, GROUP // 2)
            def _(pair):
                step(GROUP - 1 - 2 * pair, 1, k, chunks - k)
                step(GROUP - 2 - 2 * pair, 0, k, chunks - k)


def ring(count, by):
    return [(i, (i + by) % count) for i in range(count)]


def parity_order(cols):
    order = np.concatenate([np.arange(0, cols, 2), np.arange(1, cols, 2)])
    return jnp.asarray(np.eye(cols, dtype=np.float32)[:, order])


def reorder(block, matrix):
    return lax.dot_general(block, matrix, (((block.ndim - 1,), (0,)), ((), ())), precision=lax.Precision.HIGHEST)


def widen(block, axis_x, axis_y):
    n, rows, cols = block.shape
    half, quarter = cols // 2, cols // 4
    nx, ny = lax.axis_size(axis_x), lax.axis_size(axis_y)
    side = lambda start: jnp.concatenate(
        [block[..., start : start + quarter], block[..., start + half : start + half + quarter]], axis=2
    )
    pack = lambda v: jnp.concatenate([v[: n // 2], v[n // 2 :]], axis=2)
    unpack = lambda v: jnp.concatenate([v[:, :, :half], v[:, :, half:]], axis=0)
    left = unpack(lax.ppermute(pack(side(quarter)), axis_x, ring(nx, 1)))
    right = unpack(lax.ppermute(pack(side(0)), axis_x, ring(nx, -1)))
    even = jnp.concatenate([block[..., :half], right[..., :quarter], left[..., :quarter]], axis=2)
    odd = jnp.concatenate([block[..., half:], right[..., quarter:], left[..., quarter:]], axis=2)
    wide = jnp.stack([even, odd], axis=1)
    above = lax.ppermute(wide, axis_y, ring(ny, 1))
    below = lax.ppermute(wide, axis_y, ring(ny, -1))
    return above, wide, below


def pack_corners(above, wide, below):
    n, _, rows, cols = wide.shape
    half, quarter = cols // 2, cols // 4
    lane = lax.broadcasted_iota(jnp.int32, (2, rows, cols), 2)
    parity = lax.broadcasted_iota(jnp.int32, (2, rows, cols), 0)
    away = jnp.where(lane < cols - quarter, 2 * (lane - half) + 1 + parity, 2 * (cols - lane) - parity)
    own = lane < half
    from_above = own | (away <= lax.broadcasted_iota(jnp.int32, (2, rows, cols), 1))
    swapped = jnp.concatenate([below[..., :half], below[..., cols - quarter :], below[..., half : cols - quarter]], axis=3)
    upper = jnp.concatenate([jnp.where(from_above, above, swapped), wide], axis=2).reshape(n, 4 * rows, cols)
    lower = jnp.concatenate([below[:, 0, :, :half], below[:, 1, :, :half]], axis=2)
    return jnp.concatenate([upper, lower], axis=1)


AROUND = [(0, -1), (0, 1), (1, -1), (1, 0), (1, 1), (-1, -1), (-1, 0), (-1, 1)]
STRIDE = 4


def tile_at(nx, ny, dx, dy):
    tx, ty = lax.axis_index("tx"), lax.axis_index("ty")
    return lax.rem(tx + dx + nx, nx) * ny + lax.rem(ty + dy + ny, ny)


def share_kernel(nx, ny, parts_ref, index_ref, order_ref, grad_ref, vol_ref, out_ref):
    slab, rows, cols = index_ref.shape
    out_ref[...] = jnp.zeros_like(out_ref)
    for s in range(slab):
        grad = parts_ref[0, s]
        for p in range(1, parts_ref.shape[0]):
            grad = grad + parts_ref[p, s]
        grad = jnp.dot(grad, order_ref[...], precision=lax.Precision.HIGHEST, preferred_element_type=jnp.float32)
        vol = index_ref[s] - step_size * grad
        grad_ref[s] = grad
        vol_ref[s] = vol
        turned = vol.T
        keep = pl.ds(STRIDE * s, TV_STEPS)
        for dx, dy in AROUND:
            spot = tile_at(nx, ny, dx, dy)
            if dx == 0:
                out_ref[spot, keep, :] = vol[rows - TV_STEPS :] if dy > 0 else vol[:TV_STEPS]
            else:
                out_ref[spot, keep, :rows] = turned[cols - TV_STEPS :] if dx > 0 else turned[:TV_STEPS]


def sort_kernel(nx, ny, strips_ref, vol_ref, near_ref, up_ref, down_ref):
    slab, rows, cols = vol_ref.shape
    body_rows = TV_STEPS * rows
    part = STRIDE * TV_STEPS
    for s in range(TV_STEPS):
        down_ref[pl.ds(rows * s, rows), :] = vol_ref[s]
        up_ref[pl.ds(rows * s, rows), :] = vol_ref[slab - TV_STEPS + s]
    for i, (dx, dy) in enumerate(AROUND):
        strip = strips_ref[tile_at(nx, ny, dx, dy)]
        near_ref[i] = strip
        down_ref[pl.ds(body_rows + part * i, part), :] = strip[:part]
        up_ref[pl.ds(body_rows + part * i, part), :] = strip[STRIDE * (slab - TV_STEPS) :]


def smooth_kernel(nz, vol_ref, near_ref, low_ref, high_ref, out_ref, v, fz, fy, fx, turn):
    slab, rows, cols = vol_ref.shape
    body_rows = TV_STEPS * rows
    part = STRIDE * TV_STEPS
    depth = slab + 2 * TV_STEPS
    base = 16
    lane3 = lax.broadcasted_iota(jnp.int32, (TV_STEPS, cols), 1)
    first, last = lane_masks()
    turn[...] = jnp.zeros_like(turn)
    for z in range(depth):
        s = z - TV_STEPS
        if 0 <= s < slab:
            tile = vol_ref[s]
            near = [near_ref[i, pl.ds(STRIDE * s, TV_STEPS), :] for i in range(8)]
        else:
            src, k = (low_ref, z) if s < 0 else (high_ref, s - slab)
            tile = src[pl.ds(rows * k, rows), :]
            near = [src[pl.ds(body_rows + part * i + STRIDE * k, TV_STEPS), :] for i in range(8)]
        for half in range(2):
            v[z, half, pl.ds(0, base), :] = jnp.zeros((base, cols), jnp.float32)
            v[z, half, pl.ds(base + rows, 16), :] = jnp.zeros((16, cols), jnp.float32)
        v[z, 0, pl.ds(base, rows), :] = tile
        v[z, 0, pl.ds(base - TV_STEPS, TV_STEPS), :] = near[0]
        v[z, 0, pl.ds(base + rows, TV_STEPS), :] = near[1]
        for row, k in ((0, 2), (cols - TV_STEPS, 5)):
            above, beside, below = near[k : k + 3]
            ends = jnp.where(lane3 < 3 * cols // 4, pltpu.roll(below, rows, 1), pltpu.roll(above, rows, 1))
            turn[pl.ds(row, TV_STEPS), :] = jnp.where(lane3 < rows, beside, ends)
        sides = turn[...].T
        v[z, 1, pl.ds(base, rows), :] = sides[:rows]
        v[z, 1, pl.ds(base + rows, TV_STEPS), :] = sides[rows : rows + TV_STEPS]
        v[z, 1, pl.ds(base - TV_STEPS, TV_STEPS), :] = sides[cols - TV_STEPS :]

    z_first = lax.axis_index("angle") * slab - TV_STEPS + nz
    chunks = rows // 8 + 2
    for t in range(TV_STEPS):

        @pl.loop(t, depth - 1 - t)
        def _(z):
            inner = jnp.where(lax.rem(z_first + z, nz) == nz - 1, 0.0, 1.0)
            for c in range(chunks):
                row = base - 8 + 8 * c
                mid = [v[z, half, pl.ds(row, 8), :] for half in range(2)]
                ahead = [pltpu.roll(m, cols - 1, 1) for m in mid]
                for half in range(2):
                    dz = (v[z + 1, half, pl.ds(row, 8), :] - mid[half]) * inner
                    dy = v[z, half, pl.ds(row + 1, 8), :] - mid[half]
                    dx = jnp.where(last, ahead[1 - half], ahead[half]) - mid[half]
                    scale = lax.rsqrt(dz * dz + dy * dy + dx * dx + tv_smooth * tv_smooth)
                    fz[z, half, pl.ds(row, 8), :] = dz * scale
                    fy[z, half, pl.ds(row, 8), :] = dy * scale
                    fx[z, half, pl.ds(row, 8), :] = dx * scale

        @pl.loop(t + 1, depth - 1 - t)
        def _(z):
            final = t == TV_STEPS - 1
            for c in range(1, chunks - 1) if final else range(chunks):
                row = base - 8 + 8 * c
                mid = [fx[z, half, pl.ds(row, 8), :] for half in range(2)]
                behind = [pltpu.roll(m, 1, 1) for m in mid]
                for half in range(1 if final else 2):
                    here = pl.ds(row, 8)
                    div = fz[z, half, here, :] - fz[z - 1, half, here, :]
                    div = div + (fy[z, half, here, :] - fy[z, half, pl.ds(row - 1, 8), :])
                    div = div + (mid[half] - jnp.where(first, behind[1 - half], behind[half]))
                    new = v[z, half, here, :] + tv_rate * div
                    if final:
                        out_ref[z - TV_STEPS, pl.ds(row - base, 8), :] = new
                    else:
                        v[z, half, here, :] = new


def step_and_smooth(parts, index, order, nz):
    slab, rows, cols = index.shape
    nx, ny = lax.axis_size("tx"), lax.axis_size("ty")
    block = jax.ShapeDtypeStruct(index.shape, jnp.float32)
    params = pltpu.CompilerParams(vmem_limit_bytes=40 * 2**20)
    strip_rows = STRIDE * slab
    gradient, volume, strips = pl.pallas_call(
        functools.partial(share_kernel, nx, ny),
        out_shape=(block, block, jax.ShapeDtypeStruct((nx * ny, strip_rows, cols), jnp.float32)),
        compiler_params=params,
        name="share",
    )(parts, index, order)
    strips = lax.all_to_all(strips, ("tx", "ty"), 0, 0, tiled=True)
    outward = jax.ShapeDtypeStruct((TV_STEPS * (rows + 8 * STRIDE), cols), jnp.float32)
    near, up, down = pl.pallas_call(
        functools.partial(sort_kernel, nx, ny),
        out_shape=(jax.ShapeDtypeStruct((8, strip_rows, cols), jnp.float32), outward, outward),
        compiler_params=params,
        name="sort",
    )(strips, volume)
    depth = lax.axis_size("angle")
    low = lax.ppermute(up, "angle", ring(depth, 1))
    high = lax.ppermute(down, "angle", ring(depth, -1))
    whole = pltpu.VMEM((slab + 2 * TV_STEPS, 2, rows + 32, cols), jnp.float32)
    smoothed = pl.pallas_call(
        functools.partial(smooth_kernel, nz),
        out_shape=block,
        scratch_shapes=[whole, whole, whole, whole, pltpu.VMEM((cols, cols), jnp.float32)],
        compiler_params=params,
        name="smooth",
    )(volume, near, low, high)
    return gradient, smoothed


def body(index, measured, illum):
    slab, rows, cols = index.shape
    depth = lax.axis_size("angle")
    nz = slab * depth
    nx = cols * lax.axis_size("tx")
    ny = rows * lax.axis_size("ty")
    tall = 3 * rows
    core_groups = [[2 * i, 2 * i + 1] for i in range(depth // 2)]
    chip_groups = [list(range(c, depth, 2)) for c in range(2)]

    block = (2, tall, cols)
    lane = lax.broadcasted_iota(jnp.int32, block, 2)
    column = 2 * lane + lax.broadcasted_iota(jnp.int32, block, 0)
    gx = lax.axis_index("tx") * cols + jnp.where(lane < cols - cols // 4, column, column - 2 * cols)
    gy = lax.axis_index("ty") * rows - rows + lax.broadcasted_iota(jnp.int32, block, 1)
    turns = (illum[0, 0] * gx * (ny // math.gcd(nx, ny)) + illum[0, 1] * gy * (nx // math.gcd(nx, ny)))
    whole = math.lcm(nx, ny)
    turns = lax.rem(lax.rem(turns, whole) + whole, whole)
    q = (2.0 * math.pi / whole) * turns.astype(jnp.float32)
    start = jnp.stack([jnp.cos(q), jnp.sin(q)])

    order = parity_order(cols)
    column = lax.all_gather(pack_corners(*widen(reorder(index, order), "tx", "ty")), "angle", axis=0, tiled=True)

    index_block = (GROUP, 5 * rows, cols)
    field_block = (GROUP, 2, 2, rows, cols)
    steps = nz // GROUP
    scratch = [pltpu.VMEM((2, 4, tall + 16, cols), jnp.float32)]
    params = pltpu.CompilerParams(dimension_semantics=("arbitrary",), vmem_limit_bytes=50 * 2**20)
    fields = pl.pallas_call(
        functools.partial(forward_kernel, tall),
        grid=(steps,),
        in_specs=[
            pl.BlockSpec(index_block, lambda i: (i, 0, 0)),
            pl.BlockSpec((2, 2, tall, cols), lambda i: (0, 0, 0, 0)),
        ],
        out_specs=pl.BlockSpec(field_block, lambda i: (i, 0, 0, 0, 0)),
        out_shape=jax.ShapeDtypeStruct((nz, 2, 2, rows, cols), jnp.float32),
        scratch_shapes=scratch,
        compiler_params=params,
        name="forward",
    )(column, start)

    back = (TURN.conjugate() ** nz)
    back = back / abs(back)
    target = reorder(measured[:, 0], order)
    target_re = back.real * target[0] - back.imag * target[1]
    target_im = back.real * target[1] + back.imag * target[0]
    reached = fields[nz - 1]
    reached = jnp.concatenate([reached[:, 0, :, : cols // 2], reached[:, 1, :, : cols // 2]], axis=2)
    residual = reached - jnp.stack([target_re, target_im])
    adjoint = jnp.concatenate(widen(residual, "tx", "ty"), axis=2)

    grads = pl.pallas_call(
        functools.partial(backward_kernel, tall),
        grid=(steps,),
        in_specs=[
            pl.BlockSpec(index_block, lambda i: (steps - 1 - i, 0, 0)),
            pl.BlockSpec((2, 2, tall, cols), lambda i: (0, 0, 0, 0)),
            pl.BlockSpec(field_block, lambda i: (steps - 1 - i, 0, 0, 0, 0)),
        ],
        out_specs=pl.BlockSpec((2, 1, slab, rows, cols), lambda i: (0, steps - 1 - i, 0, 0, 0)),
        out_shape=jax.ShapeDtypeStruct((2, depth // 2, slab, rows, cols), jnp.float32),
        scratch_shapes=scratch,
        compiler_params=params,
        name="backward",
    )(column, adjoint, fields)

    pair = lax.all_to_all(grads, "angle", 0, 0, tiled=True, axis_index_groups=core_groups)
    both = pair[0] + pair[1]
    parts = lax.all_to_all(both, "angle", 0, 0, tiled=True, axis_index_groups=chip_groups)
    return step_and_smooth(parts, index, order.T, nz)


def solution(mesh):
    in_specs = (P("angle", "ty", "tx"), P(None, "angle", "ty", "tx"), P("angle", None))
    out_specs = (P("angle", "ty", "tx"), P("angle", "ty", "tx"))
    return jax.shard_map(body, mesh=mesh, in_specs=in_specs, out_specs=out_specs, check_vma=False)
```

```python
import functools
import math

import jax
import jax.numpy as jnp
import numpy as np
from jax import lax
from jax.experimental import pallas as pl
from jax.experimental.pallas import tpu as pltpu
from jax.sharding import PartitionSpec as P

TV_STEPS = 3
GROUP = 8

damping = 0.2
disperse = 0.1
phase_scale = 0.1
step_size = 0.1
tv_rate = 0.05
tv_smooth = 0.1

SPREAD = complex(damping, disperse)
GAIN = abs(SPREAD)
TURN = SPREAD / GAIN


def _fit():
    nodes = np.cos((np.arange(400) + 0.5) * np.pi / 400)
    t = 3.05 * (nodes + 1.0)
    z = t * t
    scaled = z / z.max()
    even = np.linalg.lstsq(scaled[:, None] ** np.arange(4), GAIN * np.cos(phase_scale * t), rcond=None)[0]
    odd = np.linalg.lstsq(scaled[:, None] ** np.arange(4), GAIN * np.sin(phase_scale * t) / t, rcond=None)[0]
    powers = z.max() ** np.arange(4)
    return [float(v) for v in even / powers], [float(v) for v in odd / powers]


EVEN, ODD = _fit()


def phase_factor(t):
    z = t * t
    cosine = EVEN[3]
    for coef in EVEN[2::-1]:
        cosine = cosine * z + coef
    sine = ODD[3]
    for coef in ODD[2::-1]:
        sine = sine * z + coef
    return cosine, sine * t


def neighbours(buf, slot, part, row, first, last):
    mid = [buf[slot, 2 * part + half, pl.ds(row, 8), :] for half in range(2)]
    low = [pltpu.roll(m, 1, 1) for m in mid]
    high = [pltpu.roll(m, 127, 1) for m in mid]
    out = []
    for half in range(2):
        left = jnp.where(first, low[1 - half], low[half])
        right = jnp.where(last, high[1 - half], high[half])
        up = buf[slot, 2 * part + half, pl.ds(row - 1, 8), :]
        down = buf[slot, 2 * part + half, pl.ds(row + 1, 8), :]
        out.append((left + right) + (up + down))
    return mid, out


def lane_masks():
    lane = lax.broadcasted_iota(jnp.int32, (8, 128), 1)
    return lane == 0, lane == 127


def near_index(near_ref, j, half, c):
    tall = near_ref.shape[1] // 2
    return near_ref[j, pl.ds(tall * half + 8 * c, 8), :]


def full_index(near_ref, far_ref, j, half, c):
    edge = far_ref.shape[1] // 3
    cn = c - edge // 8
    tall = near_ref.shape[1] // 2
    if 0 <= cn < tall // 8:
        return near_index(near_ref, j, half, cn)
    if cn < 0:
        return far_ref[j, pl.ds(2 * edge * half + 8 * c, 8), :]
    c = cn - tall // 8
    if half == 0:
        return far_ref[j, pl.ds(edge + 8 * c, 8), :]
    return pltpu.roll(far_ref[j, pl.ds(2 * edge + 8 * c, 8), :], 64, 1)


def forward_kernel(near_ref, start_ref, field_ref, last_ref, buf):
    tall = start_ref.shape[2]
    chunks = tall // 8
    own_first = (tall - field_ref.shape[2]) // 16
    own_last = chunks - own_first
    pid = pl.program_id(0)
    first, last = lane_masks()

    @pl.when(pid == 0)
    def _():
        buf[...] = jnp.zeros_like(buf)
        for q in range(4):
            buf[0, q, 8 : 8 + tall, :] = start_ref[q // 2, q % 2]

    def step(pair, odd, lo, hi):
        for c in range(lo, hi):
            row = 8 + 8 * c
            re, sum_re = neighbours(buf, odd, 0, row, first, last)
            im, sum_im = neighbours(buf, odd, 1, row, first, last)
            for half in range(2):
                cosine, sine = phase_factor(near_index(near_ref, 2 * pair + odd, half, c))
                wre = sum_re[half] + (im[half] + im[half])
                wim = sum_im[half] - (re[half] + re[half])
                nre = cosine * wre - sine * wim
                nim = cosine * wim + sine * wre
                buf[1 - odd, half, pl.ds(row, 8), :] = nre
                buf[1 - odd, 2 + half, pl.ds(row, 8), :] = nim
                if half == 0 and own_first <= c < own_last:
                    own = pl.ds(8 * (c - own_first), 8)
                    field_ref[2 * pair + odd, 0, own, :] = nre
                    field_ref[2 * pair + odd, 1, own, :] = nim

    for k in range(own_first):

        @pl.when(pid == k)
        def _(k=k):
            @pl.loop(0, GROUP // 2)
            def _(pair):
                step(pair, 0, k, chunks - k)
                step(pair, 1, k, chunks - k)

            if k == own_first - 1:
                for q in range(4):
                    last_ref[q // 2, q % 2] = buf[0, q, 8 + 8 * own_first : 8 + 8 * own_last, :]


def backward_kernel(near_ref, far_ref, start_ref, early_ref, late_ref, grad_ref, buf):
    tall = start_ref.shape[2]
    chunks = tall // 8
    own_first = (tall - early_ref.shape[2]) // 16
    own_last = chunks - own_first
    rim = own_first // 2
    pid = pl.program_id(0)
    first, last = lane_masks()
    slab = GROUP // 2

    @pl.when(pid == 0)
    def _():
        buf[...] = jnp.zeros_like(buf)

    def finish(wide, pair, odd, c, half, are, aim):
        j = 2 * pair + odd
        if half == 0 and own_first <= c < own_last:
            own = pl.ds(8 * (c - own_first), 8)
            field_ref = late_ref if wide else early_ref
            fre = field_ref[j, 0, own, :]
            fim = field_ref[j, 1, own, :]
            grad_ref[j // slab, 0, j % slab, own, :] = phase_scale * (aim * fre - are * fim)
        if wide:
            index = full_index(near_ref, far_ref, j, half, c)
        else:
            index = near_index(near_ref, j, half, c - rim)
        cosine, sine = phase_factor(index)
        row = pl.ds(8 + 8 * c, 8)
        buf[odd, half, row, :] = cosine * are + sine * aim
        buf[odd, 2 + half, row, :] = cosine * aim - sine * are

    def step(wide, pair, odd, lo, hi):
        for c in range(lo, hi):
            row = 8 + 8 * c
            re, sum_re = neighbours(buf, 1 - odd, 0, row, first, last)
            im, sum_im = neighbours(buf, 1 - odd, 1, row, first, last)
            for half in range(2):
                are = sum_re[half] - (im[half] + im[half])
                aim = sum_im[half] + (re[half] + re[half])
                finish(wide, pair, odd, c, half, are, aim)

    for k in range(own_first):

        @pl.when(pid == k)
        def _(k=k):
            wide = k < rim
            top = GROUP // 2 - 1
            if k == 0:
                for c in range(chunks):
                    for half in range(2):
                        rows = pl.ds(8 * c, 8)
                        finish(wide, top, 1, c, half, start_ref[0, half, rows, :], start_ref[1, half, rows, :])
                step(wide, top, 0, k, chunks - k)

            @pl.loop(1 if k == 0 else 0, GROUP // 2)
            def _(back):
                step(wide, top - back, 1, k, chunks - k)
                step(wide, top - back, 0, k, chunks - k)


def ring(count, by):
    return [(i, (i + by) % count) for i in range(count)]


def widen_x(block):
    n, rows, cols = block.shape
    half = cols // 2
    nx = lax.axis_size("tx")
    pack = lambda v: jnp.concatenate([v[: n // 2], v[n // 2 :]], axis=2)
    unpack = lambda v: jnp.concatenate([v[:, :, :half], v[:, :, half:]], axis=0)
    left = unpack(lax.ppermute(pack(block[:, :, half:]), "tx", ring(nx, 1)))
    right = unpack(lax.ppermute(pack(block[:, :, :half]), "tx", ring(nx, -1)))
    return jnp.stack([block, jnp.concatenate([right, left], axis=2)], axis=1)


def rows_around(wide, start, stop):
    rows = wide.shape[2]
    ny = lax.axis_size("ty")
    above = lax.ppermute(wide[:, :, rows - stop : rows - start], "ty", ring(ny, 1))
    below = lax.ppermute(wide[:, :, start:stop], "ty", ring(ny, -1))
    return above, below


def widen(block):
    wide = widen_x(block)
    above, below = rows_around(wide, 0, wide.shape[2])
    return jnp.concatenate([above, wide, below], axis=2)


def turned(block):
    return jnp.roll(block, block.shape[-1] // 2, axis=-1)


def gather_index(index):
    slab, rows, cols = index.shape
    reach = rows // 2
    lane = lax.broadcasted_iota(jnp.int32, (1, cols), 1)
    inner = (lane < cols // 4) | (lane >= cols - cols // 4)
    wide = widen_x(index)
    above, below = rows_around(wide, 0, reach)
    near = jnp.concatenate([above, wide, below], axis=2).reshape(slab, 2 * (rows + 2 * reach), cols)
    near = lax.all_gather(near, "angle", axis=0, tiled=True)
    above, below = rows_around(wide, reach, 2 * reach)
    corners = jnp.where(inner, above[:, 1], turned(below[:, 1]))
    far = jnp.concatenate([above[:, 0], below[:, 0], corners], axis=1)
    far = lax.all_gather(far, "angle", axis=0, tiled=True)
    return near, far


AROUND = [(0, -1), (0, 1), (1, -1), (1, 0), (1, 1), (-1, -1), (-1, 0), (-1, 1)]
STRIDE = 4


def tile_at(nx, ny, dx, dy):
    tx, ty = lax.axis_index("tx"), lax.axis_index("ty")
    return lax.rem(tx + dx + nx, nx) * ny + lax.rem(ty + dy + ny, ny)


def share_kernel(nx, ny, parts_ref, index_ref, grad_ref, vol_ref, out_ref):
    slab, rows, cols = index_ref.shape
    out_ref[...] = jnp.zeros_like(out_ref)
    for s in range(slab):
        grad = parts_ref[0, s]
        for p in range(1, parts_ref.shape[0]):
            grad = grad + parts_ref[p, s]
        vol = index_ref[s] - step_size * grad
        grad_ref[s] = grad
        vol_ref[s] = vol
        turned = vol.T
        keep = pl.ds(STRIDE * s, TV_STEPS)
        for dx, dy in AROUND:
            spot = tile_at(nx, ny, dx, dy)
            if dx == 0:
                out_ref[spot, keep, :] = vol[rows - TV_STEPS :] if dy > 0 else vol[:TV_STEPS]
            else:
                out_ref[spot, keep, :rows] = turned[cols - TV_STEPS :] if dx > 0 else turned[:TV_STEPS]


def sort_kernel(nx, ny, strips_ref, vol_ref, near_ref, up_ref, down_ref):
    slab, rows, cols = vol_ref.shape
    body_rows = TV_STEPS * rows
    part = STRIDE * TV_STEPS
    for s in range(TV_STEPS):
        down_ref[pl.ds(rows * s, rows), :] = vol_ref[s]
        up_ref[pl.ds(rows * s, rows), :] = vol_ref[slab - TV_STEPS + s]
    for i, (dx, dy) in enumerate(AROUND):
        strip = strips_ref[tile_at(nx, ny, dx, dy)]
        near_ref[i] = strip
        down_ref[pl.ds(body_rows + part * i, part), :] = strip[:part]
        up_ref[pl.ds(body_rows + part * i, part), :] = strip[STRIDE * (slab - TV_STEPS) :]


def smooth_kernel(nz, vol_ref, near_ref, low_ref, high_ref, out_ref, v, fz, fy, fx, turn):
    slab, rows, cols = vol_ref.shape
    body_rows = TV_STEPS * rows
    part = STRIDE * TV_STEPS
    depth = slab + 2 * TV_STEPS
    base = 16
    lane3 = lax.broadcasted_iota(jnp.int32, (TV_STEPS, cols), 1)
    first, last = lane_masks()
    turn[...] = jnp.zeros_like(turn)
    for z in range(depth):
        s = z - TV_STEPS
        if 0 <= s < slab:
            tile = vol_ref[s]
            near = [near_ref[i, pl.ds(STRIDE * s, TV_STEPS), :] for i in range(8)]
        else:
            src, k = (low_ref, z) if s < 0 else (high_ref, s - slab)
            tile = src[pl.ds(rows * k, rows), :]
            near = [src[pl.ds(body_rows + part * i + STRIDE * k, TV_STEPS), :] for i in range(8)]
        for half in range(2):
            v[z, half, pl.ds(0, base), :] = jnp.zeros((base, cols), jnp.float32)
            v[z, half, pl.ds(base + rows, 16), :] = jnp.zeros((16, cols), jnp.float32)
        v[z, 0, pl.ds(base, rows), :] = tile
        v[z, 0, pl.ds(base - TV_STEPS, TV_STEPS), :] = near[0]
        v[z, 0, pl.ds(base + rows, TV_STEPS), :] = near[1]
        for row, k in ((0, 2), (cols - TV_STEPS, 5)):
            above, beside, below = near[k : k + 3]
            ends = jnp.where(lane3 < 3 * cols // 4, pltpu.roll(below, rows, 1), pltpu.roll(above, rows, 1))
            turn[pl.ds(row, TV_STEPS), :] = jnp.where(lane3 < rows, beside, ends)
        sides = turn[...].T
        v[z, 1, pl.ds(base, rows), :] = sides[:rows]
        v[z, 1, pl.ds(base + rows, TV_STEPS), :] = sides[rows : rows + TV_STEPS]
        v[z, 1, pl.ds(base - TV_STEPS, TV_STEPS), :] = sides[cols - TV_STEPS :]

    z_first = lax.axis_index("angle") * slab - TV_STEPS + nz
    chunks = rows // 8 + 2
    for t in range(TV_STEPS):

        @pl.loop(t, depth - 1 - t)
        def _(z):
            inner = jnp.where(lax.rem(z_first + z, nz) == nz - 1, 0.0, 1.0)
            for c in range(chunks):
                row = base - 8 + 8 * c
                mid = [v[z, half, pl.ds(row, 8), :] for half in range(2)]
                ahead = [pltpu.roll(m, cols - 1, 1) for m in mid]
                for half in range(2):
                    dz = (v[z + 1, half, pl.ds(row, 8), :] - mid[half]) * inner
                    dy = v[z, half, pl.ds(row + 1, 8), :] - mid[half]
                    dx = jnp.where(last, ahead[1 - half], ahead[half]) - mid[half]
                    scale = lax.rsqrt(dz * dz + dy * dy + dx * dx + tv_smooth * tv_smooth)
                    fz[z, half, pl.ds(row, 8), :] = dz * scale
                    fy[z, half, pl.ds(row, 8), :] = dy * scale
                    fx[z, half, pl.ds(row, 8), :] = dx * scale

        @pl.loop(t + 1, depth - 1 - t)
        def _(z):
            final = t == TV_STEPS - 1
            for c in range(1, chunks - 1) if final else range(chunks):
                row = base - 8 + 8 * c
                mid = [fx[z, half, pl.ds(row, 8), :] for half in range(2)]
                behind = [pltpu.roll(m, 1, 1) for m in mid]
                for half in range(1 if final else 2):
                    here = pl.ds(row, 8)
                    div = fz[z, half, here, :] - fz[z - 1, half, here, :]
                    div = div + (fy[z, half, here, :] - fy[z, half, pl.ds(row - 1, 8), :])
                    div = div + (mid[half] - jnp.where(first, behind[1 - half], behind[half]))
                    new = v[z, half, here, :] + tv_rate * div
                    if final:
                        out_ref[z - TV_STEPS, pl.ds(row - base, 8), :] = new
                    else:
                        v[z, half, here, :] = new


def step_and_smooth(parts, index, nz):
    slab, rows, cols = index.shape
    nx, ny = lax.axis_size("tx"), lax.axis_size("ty")
    block = jax.ShapeDtypeStruct(index.shape, jnp.float32)
    params = pltpu.CompilerParams(vmem_limit_bytes=40 * 2**20)
    strip_rows = STRIDE * slab
    gradient, volume, strips = pl.pallas_call(
        functools.partial(share_kernel, nx, ny),
        out_shape=(block, block, jax.ShapeDtypeStruct((nx * ny, strip_rows, cols), jnp.float32)),
        compiler_params=params,
        name="share",
    )(parts, index)
    strips = lax.all_to_all(strips, ("tx", "ty"), 0, 0, tiled=True)
    outward = jax.ShapeDtypeStruct((TV_STEPS * (rows + 8 * STRIDE), cols), jnp.float32)
    near, up, down = pl.pallas_call(
        functools.partial(sort_kernel, nx, ny),
        out_shape=(jax.ShapeDtypeStruct((8, strip_rows, cols), jnp.float32), outward, outward),
        compiler_params=params,
        name="sort",
    )(strips, volume)
    depth = lax.axis_size("angle")
    low = lax.ppermute(up, "angle", ring(depth, 1))
    high = lax.ppermute(down, "angle", ring(depth, -1))
    whole = pltpu.VMEM((slab + 2 * TV_STEPS, 2, rows + 32, cols), jnp.float32)
    smoothed = pl.pallas_call(
        functools.partial(smooth_kernel, nz),
        out_shape=block,
        scratch_shapes=[whole, whole, whole, whole, pltpu.VMEM((cols, cols), jnp.float32)],
        compiler_params=params,
        name="smooth",
    )(volume, near, low, high)
    return gradient, smoothed


def incident(illum, shape, reach):
    rows, cols = shape
    nx = cols * lax.axis_size("tx")
    ny = rows * lax.axis_size("ty")
    block = (2, rows + 2 * reach, cols)
    half = lax.broadcasted_iota(jnp.int32, block, 0)
    lane = lax.broadcasted_iota(jnp.int32, block, 2)
    beside = jnp.where(lane < cols // 2, lane + cols, lane - cols)
    gx = lax.axis_index("tx") * cols + jnp.where(half == 0, lane, beside)
    gy = lax.axis_index("ty") * rows - reach + lax.broadcasted_iota(jnp.int32, block, 1)
    whole = math.lcm(nx, ny)
    parts = illum[0, 0] * gx * (whole // nx) + illum[0, 1] * gy * (whole // ny)
    parts = lax.rem(lax.rem(parts, whole) + whole, whole)
    q = (2.0 * math.pi / whole) * parts.astype(jnp.float32)
    return jnp.stack([jnp.cos(q), jnp.sin(q)])


def body(index, measured, illum):
    slab, rows, cols = index.shape
    depth = lax.axis_size("angle")
    nz = slab * depth
    reach = rows // 2
    core_groups = [[2 * i, 2 * i + 1] for i in range(depth // 2)]
    chip_groups = [list(range(c, depth, 2)) for c in range(2)]

    near, far = gather_index(index)

    steps = nz // GROUP
    near_block = (GROUP,) + near.shape[1:]
    far_block = (GROUP,) + far.shape[1:]
    field_block = (GROUP, 2, rows, cols)
    params = pltpu.CompilerParams(dimension_semantics=("arbitrary",), vmem_limit_bytes=61 * 2**20)

    def forward(start, first_step):
        whole = pl.BlockSpec(start.shape, lambda i: (0, 0, 0, 0))
        return pl.pallas_call(
            forward_kernel,
            grid=(steps // 2,),
            in_specs=[pl.BlockSpec(near_block, lambda i: (i + first_step, 0, 0)), whole],
            out_specs=(
                pl.BlockSpec(field_block, lambda i: (i, 0, 0, 0)),
                pl.BlockSpec((2, 2, rows, cols), lambda i: (0, 0, 0, 0)),
            ),
            out_shape=(
                jax.ShapeDtypeStruct((nz // 2, 2, rows, cols), jnp.float32),
                jax.ShapeDtypeStruct((2, 2, rows, cols), jnp.float32),
            ),
            scratch_shapes=[pltpu.VMEM((2, 4, rows + 2 * reach + 16, cols), jnp.float32)],
            compiler_params=params,
            name="forward",
        )(near, start)

    early, reached = forward(incident(illum, (rows, cols), reach), 0)
    above, below = rows_around(reached, 0, reach)
    late, reached = forward(jnp.concatenate([above, reached, below], axis=2), steps // 2)

    back = TURN.conjugate() ** nz
    back = back / abs(back)
    target_re = back.real * measured[0] - back.imag * measured[1]
    target_im = back.real * measured[1] + back.imag * measured[0]
    residual = reached[:, 0] - jnp.concatenate([target_re, target_im], axis=0)
    adjoint = widen(residual)

    grads = pl.pallas_call(
        backward_kernel,
        grid=(steps,),
        in_specs=[
            pl.BlockSpec(near_block, lambda i: (steps - 1 - i, 0, 0)),
            pl.BlockSpec(far_block, lambda i: (jnp.maximum(steps - 1 - i, steps // 2), 0, 0)),
            pl.BlockSpec(adjoint.shape, lambda i: (0, 0, 0, 0)),
            pl.BlockSpec(field_block, lambda i: (jnp.minimum(steps - 1 - i, steps // 2 - 1), 0, 0, 0)),
            pl.BlockSpec(field_block, lambda i: (jnp.maximum(steps // 2 - 1 - i, 0), 0, 0, 0)),
        ],
        out_specs=pl.BlockSpec((2, 1, slab, rows, cols), lambda i: (0, steps - 1 - i, 0, 0, 0)),
        out_shape=jax.ShapeDtypeStruct((2, depth // 2, slab, rows, cols), jnp.float32),
        scratch_shapes=[pltpu.VMEM((2, 4, 3 * rows + 16, cols), jnp.float32)],
        compiler_params=params,
        name="backward",
    )(near, far, adjoint, early, late)

    pair = lax.all_to_all(grads, "angle", 0, 0, tiled=True, axis_index_groups=core_groups)
    both = pair[0] + pair[1]
    parts = lax.all_to_all(both, "angle", 0, 0, tiled=True, axis_index_groups=chip_groups)
    return step_and_smooth(parts, index, nz)


def solution(mesh):
    in_specs = (P("angle", "ty", "tx"), P(None, "angle", "ty", "tx"), P("angle", None))
    out_specs = (P("angle", "ty", "tx"), P("angle", "ty", "tx"))
    return jax.shard_map(body, mesh=mesh, in_specs=in_specs, out_specs=out_specs, check_vma=False)
```

```python
import functools
import math

import jax
import jax.numpy as jnp
import numpy as np
from jax import lax
from jax.experimental import pallas as pl
from jax.experimental.pallas import tpu as pltpu
from jax.sharding import PartitionSpec as P

TV_STEPS = 3
HALO = 64
GROUP = 8

damping = 0.2
disperse = 0.1
phase_scale = 0.1
step_size = 0.1
tv_rate = 0.05
tv_smooth = 0.1

SPREAD = complex(damping, disperse)
GAIN = abs(SPREAD)
TURN = SPREAD / GAIN


def _fit():
    nodes = np.cos((np.arange(400) + 0.5) * np.pi / 400)
    t = 3.05 * (nodes + 1.0)
    z = t * t
    scaled = z / z.max()
    even = np.linalg.lstsq(scaled[:, None] ** np.arange(4), GAIN * np.cos(phase_scale * t), rcond=None)[0]
    odd = np.linalg.lstsq(scaled[:, None] ** np.arange(4), GAIN * np.sin(phase_scale * t) / t, rcond=None)[0]
    powers = z.max() ** np.arange(4)
    return [float(v) for v in even / powers], [float(v) for v in odd / powers]


EVEN, ODD = _fit()


def phase_factor(t):
    z = t * t
    cosine = EVEN[3]
    for coef in EVEN[2::-1]:
        cosine = cosine * z + coef
    sine = ODD[3]
    for coef in ODD[2::-1]:
        sine = sine * z + coef
    return cosine, sine * t


def neighbours(buf, slot, part, row):
    even, odd = [buf[slot, 2 * part + parity, pl.ds(row, 8), :] for parity in range(2)]
    sides = (odd + pltpu.roll(odd, 1, 1), even + pltpu.roll(even, 127, 1))
    out = []
    for parity in range(2):
        up = buf[slot, 2 * part + parity, pl.ds(row - 1, 8), :]
        down = buf[slot, 2 * part + parity, pl.ds(row + 1, 8), :]
        out.append(sides[parity] + (up + down))
    return (even, odd), out


def index_rows(index_ref, j, parity, c, chunks):
    third = chunks // 3
    rows = index_ref.shape[1] // 5
    if c < 2 * third:
        return index_ref[j, pl.ds(2 * rows * parity + 8 * c, 8), :]
    c = c - 2 * third
    corner = index_ref[j, pl.ds(2 * rows * parity + 8 * c, 8), :]
    own = index_ref[j, pl.ds(4 * rows + 8 * c, 8), :]
    if parity:
        own = pltpu.roll(own, 64, 1)
    lane = lax.broadcasted_iota(jnp.int32, (8, 128), 1)
    corner = jnp.where(lane < 96, pltpu.roll(corner, 96, 1), pltpu.roll(corner, 32, 1))
    return jnp.where(lane < 64, own, corner)


def both_parities(even, odd):
    lane = lax.broadcasted_iota(jnp.int32, (8, 128), 1)
    return jnp.where(lane < 64, even, pltpu.roll(odd, 64, 1))


def lane_masks():
    lane = lax.broadcasted_iota(jnp.int32, (8, 128), 1)
    return lane == 0, lane == 127


def forward_kernel(rows, index_ref, start_ref, field_ref, buf):
    chunks = rows // 8
    pid = pl.program_id(0)

    @pl.when(pid == 0)
    def _():
        buf[...] = jnp.zeros_like(buf)
        for q in range(4):
            buf[0, q, 8 : 8 + rows, :] = start_ref[q // 2, q % 2]

    def step(j, parity, lo, hi):
        for c in range(lo, hi):
            row = 8 + 8 * c
            re, sum_re = neighbours(buf, parity, 0, row)
            im, sum_im = neighbours(buf, parity, 1, row)
            for half in range(2):
                cosine, sine = phase_factor(index_rows(index_ref, j, half, c, chunks))
                wre = sum_re[half] + (im[half] + im[half])
                wim = sum_im[half] - (re[half] + re[half])
                nre = cosine * wre - sine * wim
                nim = cosine * wim + sine * wre
                buf[1 - parity, half, pl.ds(row, 8), :] = nre
                buf[1 - parity, 2 + half, pl.ds(row, 8), :] = nim
        for c in range(chunks // 3, 2 * chunks // 3):
            row = pl.ds(8 + 8 * c, 8)
            own = pl.ds(8 * (c - chunks // 3), 8)
            for part in range(2):
                even, odd = (buf[1 - parity, 2 * part + half, row, :] for half in range(2))
                field_ref[j, part, own, :] = both_parities(even, odd)

    for k in range(8):

        @pl.when(pid == k)
        def _(k=k):
            @pl.loop(0, GROUP // 2)
            def _(pair):
                step(2 * pair, 0, k, chunks - k)
                step(2 * pair + 1, 1, k, chunks - k)


def backward_kernel(rows, index_ref, start_ref, field_ref, grad_ref, buf, here):
    chunks = rows // 8
    pid = pl.program_id(0)
    core = lax.rem(lax.axis_index("angle"), 2)

    @pl.when(pid == 0)
    def _():
        buf[...] = jnp.zeros_like(buf)

    def finish(j, slot, c, are, aim):
        if chunks // 3 <= c < 2 * chunks // 3:
            own = pl.ds(8 * (c - chunks // 3), 8)
            for half in range(2):
                here[half, own, :] = are[half]
                here[2 + half, own, :] = aim[half]
        row = 8 + 8 * c
        for half in range(2):
            cosine, sine = phase_factor(index_rows(index_ref, j, half, c, chunks))
            buf[slot, half, pl.ds(row, 8), :] = cosine * are[half] + sine * aim[half]
            buf[slot, 2 + half, pl.ds(row, 8), :] = cosine * aim[half] - sine * are[half]

    def multiply(j):
        slab = GROUP // 2
        spot = lax.rem(j // slab + core, 2)
        for c in range(chunks // 3):
            own = pl.ds(8 * c, 8)
            are = both_parities(here[0, own, :], here[1, own, :])
            aim = both_parities(here[2, own, :], here[3, own, :])
            grad = aim * field_ref[j, 0, own, :] - are * field_ref[j, 1, own, :]
            grad_ref[spot, 0, j % slab, own, :] = phase_scale * grad

    def step(j, parity, lo, hi):
        for c in range(lo, hi):
            row = 8 + 8 * c
            re, sum_re = neighbours(buf, 1 - parity, 0, row)
            im, sum_im = neighbours(buf, 1 - parity, 1, row)
            are = [sum_re[half] - (im[half] + im[half]) for half in range(2)]
            aim = [sum_im[half] + (re[half] + re[half]) for half in range(2)]
            finish(j, parity, c, are, aim)
        multiply(j)

    for k in range(8):

        @pl.when(pid == k)
        def _(k=k):
            skip = 0
            if k == 0:
                skip = 1
                for c in range(chunks):
                    row = pl.ds(8 * c, 8)
                    finish(
                        GROUP - 1,
                        1,
                        c,
                        [start_ref[0, half, row, :] for half in range(2)],
                        [start_ref[1, half, row, :] for half in range(2)],
                    )
                multiply(GROUP - 1)
                step(GROUP - 2, 0, k, chunks - k)

            @pl.loop(skip, GROUP // 2)
            def _(pair):
                step(GROUP - 1 - 2 * pair, 1, k, chunks - k)
                step(GROUP - 2 - 2 * pair, 0, k, chunks - k)


def ring(count, by):
    return [(i, (i + by) % count) for i in range(count)]


def parity_order(cols):
    order = np.concatenate([np.arange(0, cols, 2), np.arange(1, cols, 2)])
    return jnp.asarray(np.eye(cols, dtype=np.float32)[:, order])


def reorder(block, matrix):
    return lax.dot_general(block, matrix, (((block.ndim - 1,), (0,)), ((), ())), precision=lax.Precision.HIGHEST)


def widen(block, axis_x, axis_y):
    n, rows, cols = block.shape
    half, quarter = cols // 2, cols // 4
    nx, ny = lax.axis_size(axis_x), lax.axis_size(axis_y)
    side = lambda start: jnp.concatenate(
        [block[..., start : start + quarter], block[..., start + half : start + half + quarter]], axis=2
    )
    pack = lambda v: jnp.concatenate([v[: n // 2], v[n // 2 :]], axis=2)
    unpack = lambda v: jnp.concatenate([v[:, :, :half], v[:, :, half:]], axis=0)
    left = unpack(lax.ppermute(pack(side(quarter)), axis_x, ring(nx, 1)))
    right = unpack(lax.ppermute(pack(side(0)), axis_x, ring(nx, -1)))
    even = jnp.concatenate([block[..., :half], right[..., :quarter], left[..., :quarter]], axis=2)
    odd = jnp.concatenate([block[..., half:], right[..., quarter:], left[..., quarter:]], axis=2)
    wide = jnp.stack([even, odd], axis=1)
    above = lax.ppermute(wide, axis_y, ring(ny, 1))
    below = lax.ppermute(wide, axis_y, ring(ny, -1))
    return above, wide, below


def pack_corners(above, wide, below):
    n, _, rows, cols = wide.shape
    half, quarter = cols // 2, cols // 4
    lane = lax.broadcasted_iota(jnp.int32, (2, rows, cols), 2)
    parity = lax.broadcasted_iota(jnp.int32, (2, rows, cols), 0)
    away = jnp.where(lane < cols - quarter, 2 * (lane - half) + 1 + parity, 2 * (cols - lane) - parity)
    own = lane < half
    from_above = own | (away <= lax.broadcasted_iota(jnp.int32, (2, rows, cols), 1))
    swapped = jnp.concatenate([below[..., :half], below[..., cols - quarter :], below[..., half : cols - quarter]], axis=3)
    upper = jnp.concatenate([jnp.where(from_above, above, swapped), wide], axis=2).reshape(n, 4 * rows, cols)
    lower = jnp.concatenate([below[:, 0, :, :half], below[:, 1, :, :half]], axis=2)
    return jnp.concatenate([upper, lower], axis=1)


AROUND = [(0, -1), (0, 1), (1, -1), (1, 0), (1, 1), (-1, -1), (-1, 0), (-1, 1)]
STRIDE = 4


def tile_at(nx, ny, dx, dy):
    tx, ty = lax.axis_index("tx"), lax.axis_index("ty")
    return lax.rem(tx + dx + nx, nx) * ny + lax.rem(ty + dy + ny, ny)


def share_kernel(nx, ny, parts_ref, index_ref, order_ref, grad_ref, vol_ref, out_ref):
    slab, rows, cols = index_ref.shape
    out_ref[...] = jnp.zeros_like(out_ref)
    for s in range(slab):
        grad = parts_ref[0, s]
        for p in range(1, parts_ref.shape[0]):
            grad = grad + parts_ref[p, s]
        grad = jnp.dot(grad, order_ref[...], precision=lax.Precision.HIGHEST, preferred_element_type=jnp.float32)
        vol = index_ref[s] - step_size * grad
        grad_ref[s] = grad
        vol_ref[s] = vol
        turned = vol.T
        keep = pl.ds(STRIDE * s, TV_STEPS)
        for dx, dy in AROUND:
            spot = tile_at(nx, ny, dx, dy)
            if dx == 0:
                out_ref[spot, keep, :] = vol[rows - TV_STEPS :] if dy > 0 else vol[:TV_STEPS]
            else:
                out_ref[spot, keep, :rows] = turned[cols - TV_STEPS :] if dx > 0 else turned[:TV_STEPS]


def sort_kernel(nx, ny, strips_ref, vol_ref, near_ref, up_ref, down_ref):
    slab, rows, cols = vol_ref.shape
    body_rows = TV_STEPS * rows
    part = STRIDE * TV_STEPS
    for s in range(TV_STEPS):
        down_ref[pl.ds(rows * s, rows), :] = vol_ref[s]
        up_ref[pl.ds(rows * s, rows), :] = vol_ref[slab - TV_STEPS + s]
    for i, (dx, dy) in enumerate(AROUND):
        strip = strips_ref[tile_at(nx, ny, dx, dy)]
        near_ref[i] = strip
        down_ref[pl.ds(body_rows + part * i, part), :] = strip[:part]
        up_ref[pl.ds(body_rows + part * i, part), :] = strip[STRIDE * (slab - TV_STEPS) :]


def smooth_kernel(nz, vol_ref, near_ref, low_ref, high_ref, out_ref, v, fz, fy, fx, turn):
    slab, rows, cols = vol_ref.shape
    body_rows = TV_STEPS * rows
    part = STRIDE * TV_STEPS
    depth = slab + 2 * TV_STEPS
    base = 16
    lane3 = lax.broadcasted_iota(jnp.int32, (TV_STEPS, cols), 1)
    first, last = lane_masks()
    turn[...] = jnp.zeros_like(turn)
    for z in range(depth):
        s = z - TV_STEPS
        if 0 <= s < slab:
            tile = vol_ref[s]
            near = [near_ref[i, pl.ds(STRIDE * s, TV_STEPS), :] for i in range(8)]
        else:
            src, k = (low_ref, z) if s < 0 else (high_ref, s - slab)
            tile = src[pl.ds(rows * k, rows), :]
            near = [src[pl.ds(body_rows + part * i + STRIDE * k, TV_STEPS), :] for i in range(8)]
        for half in range(2):
            v[z, half, pl.ds(0, base), :] = jnp.zeros((base, cols), jnp.float32)
            v[z, half, pl.ds(base + rows, 16), :] = jnp.zeros((16, cols), jnp.float32)
        v[z, 0, pl.ds(base, rows), :] = tile
        v[z, 0, pl.ds(base - TV_STEPS, TV_STEPS), :] = near[0]
        v[z, 0, pl.ds(base + rows, TV_STEPS), :] = near[1]
        for row, k in ((0, 2), (cols - TV_STEPS, 5)):
            above, beside, below = near[k : k + 3]
            ends = jnp.where(lane3 < 3 * cols // 4, pltpu.roll(below, rows, 1), pltpu.roll(above, rows, 1))
            turn[pl.ds(row, TV_STEPS), :] = jnp.where(lane3 < rows, beside, ends)
        sides = turn[...].T
        v[z, 1, pl.ds(base, rows), :] = sides[:rows]
        v[z, 1, pl.ds(base + rows, TV_STEPS), :] = sides[rows : rows + TV_STEPS]
        v[z, 1, pl.ds(base - TV_STEPS, TV_STEPS), :] = sides[cols - TV_STEPS :]

    z_first = lax.axis_index("angle") * slab - TV_STEPS + nz
    chunks = rows // 8 + 2
    for t in range(TV_STEPS):

        @pl.loop(t, depth - 1 - t)
        def _(z):
            inner = jnp.where(lax.rem(z_first + z, nz) == nz - 1, 0.0, 1.0)
            for c in range(chunks - 1 if t == TV_STEPS - 1 else chunks):
                row = base - 8 + 8 * c
                mid = [v[z, half, pl.ds(row, 8), :] for half in range(2)]
                ahead = [pltpu.roll(m, cols - 1, 1) for m in mid]
                for half in range(2):
                    dz = (v[z + 1, half, pl.ds(row, 8), :] - mid[half]) * inner
                    dy = v[z, half, pl.ds(row + 1, 8), :] - mid[half]
                    dx = jnp.where(last, ahead[1 - half], ahead[half]) - mid[half]
                    scale = lax.rsqrt(dz * dz + dy * dy + dx * dx + tv_smooth * tv_smooth)
                    if half == 0 or t < TV_STEPS - 1:
                        fz[z, half, pl.ds(row, 8), :] = dz * scale
                        fy[z, half, pl.ds(row, 8), :] = dy * scale
                    fx[z, half, pl.ds(row, 8), :] = dx * scale

        @pl.loop(t + 1, depth - 1 - t)
        def _(z):
            final = t == TV_STEPS - 1
            for c in range(1, chunks - 1) if final else range(chunks):
                row = base - 8 + 8 * c
                mid = [fx[z, half, pl.ds(row, 8), :] for half in range(2)]
                behind = [pltpu.roll(m, 1, 1) for m in mid]
                for half in range(1 if final else 2):
                    here = pl.ds(row, 8)
                    div = fz[z, half, here, :] - fz[z - 1, half, here, :]
                    div = div + (fy[z, half, here, :] - fy[z, half, pl.ds(row - 1, 8), :])
                    div = div + (mid[half] - jnp.where(first, behind[1 - half], behind[half]))
                    new = v[z, half, here, :] + tv_rate * div
                    if final:
                        out_ref[z - TV_STEPS, pl.ds(row - base, 8), :] = new
                    else:
                        v[z, half, here, :] = new


def step_and_smooth(parts, index, order, nz):
    slab, rows, cols = index.shape
    nx, ny = lax.axis_size("tx"), lax.axis_size("ty")
    block = jax.ShapeDtypeStruct(index.shape, jnp.float32)
    params = pltpu.CompilerParams(vmem_limit_bytes=40 * 2**20)
    strip_rows = STRIDE * slab
    gradient, volume, strips = pl.pallas_call(
        functools.partial(share_kernel, nx, ny),
        out_shape=(block, block, jax.ShapeDtypeStruct((nx * ny, strip_rows, cols), jnp.float32)),
        compiler_params=params,
        name="share",
    )(parts, index, order)
    strips = lax.all_to_all(strips, ("tx", "ty"), 0, 0, tiled=True)
    outward = jax.ShapeDtypeStruct((TV_STEPS * (rows + 8 * STRIDE), cols), jnp.float32)
    near, up, down = pl.pallas_call(
        functools.partial(sort_kernel, nx, ny),
        out_shape=(jax.ShapeDtypeStruct((8, strip_rows, cols), jnp.float32), outward, outward),
        compiler_params=params,
        name="sort",
    )(strips, volume)
    depth = lax.axis_size("angle")
    low = lax.ppermute(up, "angle", ring(depth, 1))
    high = lax.ppermute(down, "angle", ring(depth, -1))
    whole = pltpu.VMEM((slab + 2 * TV_STEPS, 2, rows + 32, cols), jnp.float32)
    smoothed = pl.pallas_call(
        functools.partial(smooth_kernel, nz),
        out_shape=block,
        scratch_shapes=[whole, whole, whole, whole, pltpu.VMEM((cols, cols), jnp.float32)],
        compiler_params=params,
        name="smooth",
    )(volume, near, low, high)
    return gradient, smoothed


def body(index, measured, illum):
    slab, rows, cols = index.shape
    depth = lax.axis_size("angle")
    nz = slab * depth
    nx = cols * lax.axis_size("tx")
    ny = rows * lax.axis_size("ty")
    tall = 3 * rows
    chip_groups = [list(range(c, depth, 2)) for c in range(2)]

    block = (2, tall, cols)
    lane = lax.broadcasted_iota(jnp.int32, block, 2)
    column = 2 * lane + lax.broadcasted_iota(jnp.int32, block, 0)
    gx = lax.axis_index("tx") * cols + jnp.where(lane < cols - cols // 4, column, column - 2 * cols)
    gy = lax.axis_index("ty") * rows - rows + lax.broadcasted_iota(jnp.int32, block, 1)
    turns = (illum[0, 0] * gx * (ny // math.gcd(nx, ny)) + illum[0, 1] * gy * (nx // math.gcd(nx, ny)))
    whole = math.lcm(nx, ny)
    turns = lax.rem(lax.rem(turns, whole) + whole, whole)
    q = (2.0 * math.pi / whole) * turns.astype(jnp.float32)
    start = jnp.stack([jnp.cos(q), jnp.sin(q)])

    order = parity_order(cols)
    column = lax.all_gather(pack_corners(*widen(reorder(index, order), "tx", "ty")), "angle", axis=0, tiled=True)

    index_block = (GROUP, 5 * rows, cols)
    field_block = (GROUP, 2, rows, cols)
    steps = nz // GROUP
    scratch = [pltpu.VMEM((2, 4, tall + 16, cols), jnp.float32)]
    params = pltpu.CompilerParams(dimension_semantics=("arbitrary",), vmem_limit_bytes=40 * 2**20)
    fields = pl.pallas_call(
        functools.partial(forward_kernel, tall),
        grid=(steps,),
        in_specs=[
            pl.BlockSpec(index_block, lambda i: (i, 0, 0)),
            pl.BlockSpec((2, 2, tall, cols), lambda i: (0, 0, 0, 0)),
        ],
        out_specs=pl.BlockSpec(field_block, lambda i: (i, 0, 0, 0)),
        out_shape=jax.ShapeDtypeStruct((nz, 2, rows, cols), jnp.float32),
        scratch_shapes=scratch,
        compiler_params=params,
        name="forward",
    )(column, start)

    back = (TURN.conjugate() ** nz)
    back = back / abs(back)
    target = reorder(measured[:, 0], order)
    target_re = back.real * target[0] - back.imag * target[1]
    target_im = back.real * target[1] + back.imag * target[0]
    residual = fields[nz - 1] - jnp.stack([target_re, target_im])
    adjoint = jnp.concatenate(widen(residual, "tx", "ty"), axis=2)

    grads = pl.pallas_call(
        functools.partial(backward_kernel, tall),
        grid=(steps,),
        in_specs=[
            pl.BlockSpec(index_block, lambda i: (steps - 1 - i, 0, 0)),
            pl.BlockSpec((2, 2, tall, cols), lambda i: (0, 0, 0, 0)),
            pl.BlockSpec(field_block, lambda i: (steps - 1 - i, 0, 0, 0)),
        ],
        out_specs=pl.BlockSpec((2, 1, slab, rows, cols), lambda i: (0, steps - 1 - i, 0, 0, 0)),
        out_shape=jax.ShapeDtypeStruct((2, depth // 2, slab, rows, cols), jnp.float32),
        scratch_shapes=scratch + [pltpu.VMEM((4, rows, cols), jnp.float32)],
        compiler_params=params,
        name="backward",
    )(column, adjoint, fields)

    both = grads[0] + lax.ppermute(grads[1], "angle", [(i, i ^ 1) for i in range(depth)])
    parts = lax.all_to_all(both, "angle", 0, 0, tiled=True, axis_index_groups=chip_groups)
    return step_and_smooth(parts, index, order.T, nz)


def solution(mesh):
    in_specs = (P("angle", "ty", "tx"), P(None, "angle", "ty", "tx"), P("angle", None))
    out_specs = (P("angle", "ty", "tx"), P("angle", "ty", "tx"))
    return jax.shard_map(body, mesh=mesh, in_specs=in_specs, out_specs=out_specs, check_vma=False)
```

```python
import functools
import math

import jax
import jax.numpy as jnp
import numpy as np
from jax import lax
from jax.experimental import pallas as pl
from jax.experimental.pallas import tpu as pltpu
from jax.sharding import PartitionSpec as P

TV_STEPS = 3
HALO = 64
GROUP = 8

damping = 0.2
disperse = 0.1
phase_scale = 0.1
step_size = 0.1
tv_rate = 0.05
tv_smooth = 0.1

SPREAD = complex(damping, disperse)
GAIN = abs(SPREAD)
TURN = SPREAD / GAIN


def _fit():
    nodes = np.cos((np.arange(400) + 0.5) * np.pi / 400)
    t = 3.05 * (nodes + 1.0)
    z = t * t
    scaled = z / z.max()
    even = np.linalg.lstsq(scaled[:, None] ** np.arange(4), GAIN * np.cos(phase_scale * t), rcond=None)[0]
    odd = np.linalg.lstsq(scaled[:, None] ** np.arange(4), GAIN * np.sin(phase_scale * t) / t, rcond=None)[0]
    powers = z.max() ** np.arange(4)
    return [float(v) for v in even / powers], [float(v) for v in odd / powers]


EVEN, ODD = _fit()


def phase_factor(t):
    z = t * t
    cosine = EVEN[3]
    for coef in EVEN[2::-1]:
        cosine = cosine * z + coef
    sine = ODD[3]
    for coef in ODD[2::-1]:
        sine = sine * z + coef
    return cosine, sine * t


def neighbours(buf, slot, part, row):
    even, odd = [buf[slot, 2 * part + parity, pl.ds(row, 8), :] for parity in range(2)]
    sides = (odd + pltpu.roll(odd, 1, 1), even + pltpu.roll(even, 127, 1))
    out = []
    for parity in range(2):
        up = buf[slot, 2 * part + parity, pl.ds(row - 1, 8), :]
        down = buf[slot, 2 * part + parity, pl.ds(row + 1, 8), :]
        out.append(sides[parity] + (up + down))
    return (even, odd), out


def index_rows(index_ref, j, parity, c, chunks):
    third = chunks // 3
    rows = index_ref.shape[1] // 5
    if c < 2 * third:
        return index_ref[j, pl.ds(2 * rows * parity + 8 * c, 8), :]
    c = c - 2 * third
    corner = index_ref[j, pl.ds(2 * rows * parity + 8 * c, 8), :]
    own = index_ref[j, pl.ds(4 * rows + 8 * c, 8), :]
    if parity:
        own = pltpu.roll(own, 64, 1)
    lane = lax.broadcasted_iota(jnp.int32, (8, 128), 1)
    corner = jnp.where(lane < 96, pltpu.roll(corner, 96, 1), pltpu.roll(corner, 32, 1))
    return jnp.where(lane < 64, own, corner)


def both_parities(even, odd):
    lane = lax.broadcasted_iota(jnp.int32, (8, 128), 1)
    return jnp.where(lane < 64, even, pltpu.roll(odd, 64, 1))


def lane_masks():
    lane = lax.broadcasted_iota(jnp.int32, (8, 128), 1)
    return lane == 0, lane == 127


def forward_kernel(rows, index_ref, start_ref, field_ref, buf):
    chunks = rows // 8
    pid = pl.program_id(0)

    @pl.when(pid == 0)
    def _():
        buf[...] = jnp.zeros_like(buf)
        for q in range(4):
            buf[0, q, 8 : 8 + rows, :] = start_ref[q // 2, q % 2]

    def step(j, parity, lo, hi):
        for c in range(lo, hi):
            row = 8 + 8 * c
            re, sum_re = neighbours(buf, parity, 0, row)
            im, sum_im = neighbours(buf, parity, 1, row)
            for half in range(2):
                cosine, sine = phase_factor(index_rows(index_ref, j, half, c, chunks))
                wre = sum_re[half] + (im[half] + im[half])
                wim = sum_im[half] - (re[half] + re[half])
                nre = cosine * wre - sine * wim
                nim = cosine * wim + sine * wre
                buf[1 - parity, half, pl.ds(row, 8), :] = nre
                buf[1 - parity, 2 + half, pl.ds(row, 8), :] = nim
        for c in range(chunks // 3, 2 * chunks // 3):
            row = pl.ds(8 + 8 * c, 8)
            own = pl.ds(8 * (c - chunks // 3), 8)
            for part in range(2):
                even, odd = (buf[1 - parity, 2 * part + half, row, :] for half in range(2))
                field_ref[j, part, own, :] = both_parities(even, odd)

    for k in range(8):

        @pl.when(pid == k)
        def _(k=k):
            @pl.loop(0, GROUP // 2)
            def _(pair):
                step(2 * pair, 0, k, chunks - k)
                step(2 * pair + 1, 1, k, chunks - k)


def backward_kernel(rows, index_ref, start_ref, field_ref, grad_ref, buf, here):
    chunks = rows // 8
    pid = pl.program_id(0)
    core = lax.rem(lax.axis_index("angle"), 2)

    @pl.when(pid == 0)
    def _():
        buf[...] = jnp.zeros_like(buf)

    def finish(j, slot, c, are, aim):
        if chunks // 3 <= c < 2 * chunks // 3:
            own = pl.ds(8 * (c - chunks // 3), 8)
            for half in range(2):
                here[half, own, :] = are[half]
                here[2 + half, own, :] = aim[half]
        row = 8 + 8 * c
        for half in range(2):
            cosine, sine = phase_factor(index_rows(index_ref, j, half, c, chunks))
            buf[slot, half, pl.ds(row, 8), :] = cosine * are[half] + sine * aim[half]
            buf[slot, 2 + half, pl.ds(row, 8), :] = cosine * aim[half] - sine * are[half]

    def multiply(j):
        slab = GROUP // 2
        spot = lax.rem(j // slab + core, 2)
        for c in range(chunks // 3):
            own = pl.ds(8 * c, 8)
            are = both_parities(here[0, own, :], here[1, own, :])
            aim = both_parities(here[2, own, :], here[3, own, :])
            grad = aim * field_ref[j, 0, own, :] - are * field_ref[j, 1, own, :]
            grad_ref[spot, 0, j % slab, own, :] = phase_scale * grad

    def step(j, parity, lo, hi):
        for c in range(lo, hi):
            row = 8 + 8 * c
            re, sum_re = neighbours(buf, 1 - parity, 0, row)
            im, sum_im = neighbours(buf, 1 - parity, 1, row)
            are = [sum_re[half] - (im[half] + im[half]) for half in range(2)]
            aim = [sum_im[half] + (re[half] + re[half]) for half in range(2)]
            finish(j, parity, c, are, aim)
        multiply(j)

    for k in range(8):

        @pl.when(pid == k)
        def _(k=k):
            skip = 0
            if k == 0:
                skip = 1
                for c in range(chunks):
                    row = pl.ds(8 * c, 8)
                    finish(
                        GROUP - 1,
                        1,
                        c,
                        [start_ref[0, half, row, :] for half in range(2)],
                        [start_ref[1, half, row, :] for half in range(2)],
                    )
                multiply(GROUP - 1)
                step(GROUP - 2, 0, k, chunks - k)

            @pl.loop(skip, GROUP // 2)
            def _(pair):
                step(GROUP - 1 - 2 * pair, 1, k, chunks - k)
                step(GROUP - 2 - 2 * pair, 0, k, chunks - k)


def ring(count, by):
    return [(i, (i + by) % count) for i in range(count)]


def parity_order(cols):
    order = np.concatenate([np.arange(0, cols, 2), np.arange(1, cols, 2)])
    return jnp.asarray(np.eye(cols, dtype=np.float32)[:, order])


def reorder(block, matrix):
    return lax.dot_general(block, matrix, (((block.ndim - 1,), (0,)), ((), ())), precision=lax.Precision.HIGHEST)


def widen(block, axis_x, axis_y):
    n, rows, cols = block.shape
    half, quarter = cols // 2, cols // 4
    nx, ny = lax.axis_size(axis_x), lax.axis_size(axis_y)
    side = lambda start: jnp.concatenate(
        [block[..., start : start + quarter], block[..., start + half : start + half + quarter]], axis=2
    )
    pack = lambda v: jnp.concatenate([v[: n // 2], v[n // 2 :]], axis=2)
    unpack = lambda v: jnp.concatenate([v[:, :, :half], v[:, :, half:]], axis=0)
    left = unpack(lax.ppermute(pack(side(quarter)), axis_x, ring(nx, 1)))
    right = unpack(lax.ppermute(pack(side(0)), axis_x, ring(nx, -1)))
    even = jnp.concatenate([block[..., :half], right[..., :quarter], left[..., :quarter]], axis=2)
    odd = jnp.concatenate([block[..., half:], right[..., quarter:], left[..., quarter:]], axis=2)
    wide = jnp.stack([even, odd], axis=1)
    above = lax.ppermute(wide, axis_y, ring(ny, 1))
    below = lax.ppermute(wide, axis_y, ring(ny, -1))
    return above, wide, below


def pack_corners(above, wide, below):
    n, _, rows, cols = wide.shape
    half, quarter = cols // 2, cols // 4
    lane = lax.broadcasted_iota(jnp.int32, (2, rows, cols), 2)
    parity = lax.broadcasted_iota(jnp.int32, (2, rows, cols), 0)
    away = jnp.where(lane < cols - quarter, 2 * (lane - half) + 1 + parity, 2 * (cols - lane) - parity)
    own = lane < half
    from_above = own | (away <= lax.broadcasted_iota(jnp.int32, (2, rows, cols), 1))
    swapped = jnp.concatenate([below[..., :half], below[..., cols - quarter :], below[..., half : cols - quarter]], axis=3)
    upper = jnp.concatenate([jnp.where(from_above, above, swapped), wide], axis=2).reshape(n, 4 * rows, cols)
    lower = jnp.concatenate([below[:, 0, :, :half], below[:, 1, :, :half]], axis=2)
    return jnp.concatenate([upper, lower], axis=1)


AROUND = [(0, -1), (0, 1), (1, -1), (1, 0), (1, 1), (-1, -1), (-1, 0), (-1, 1)]
STRIDE = 4


def tile_at(nx, ny, dx, dy):
    tx, ty = lax.axis_index("tx"), lax.axis_index("ty")
    return lax.rem(tx + dx + nx, nx) * ny + lax.rem(ty + dy + ny, ny)


def share_kernel(nx, ny, parts_ref, index_ref, order_ref, grad_ref, vol_ref, out_ref):
    slab, rows, cols = index_ref.shape
    out_ref[...] = jnp.zeros_like(out_ref)
    for s in range(slab):
        grad = parts_ref[0, s]
        for p in range(1, parts_ref.shape[0]):
            grad = grad + parts_ref[p, s]
        grad = jnp.dot(grad, order_ref[...], precision=lax.Precision.HIGHEST, preferred_element_type=jnp.float32)
        vol = index_ref[s] - step_size * grad
        grad_ref[s] = grad
        vol_ref[s] = vol
        turned = vol.T
        keep = pl.ds(STRIDE * s, TV_STEPS)
        for dx, dy in AROUND:
            spot = tile_at(nx, ny, dx, dy)
            if dx == 0:
                out_ref[spot, keep, :] = vol[rows - TV_STEPS :] if dy > 0 else vol[:TV_STEPS]
            else:
                out_ref[spot, keep, :rows] = turned[cols - TV_STEPS :] if dx > 0 else turned[:TV_STEPS]


def sort_kernel(nx, ny, strips_ref, vol_ref, near_ref, up_ref, down_ref):
    slab, rows, cols = vol_ref.shape
    body_rows = TV_STEPS * rows
    part = STRIDE * TV_STEPS
    for s in range(TV_STEPS):
        down_ref[pl.ds(rows * s, rows), :] = vol_ref[s]
        up_ref[pl.ds(rows * s, rows), :] = vol_ref[slab - TV_STEPS + s]
    for i, (dx, dy) in enumerate(AROUND):
        strip = strips_ref[tile_at(nx, ny, dx, dy)]
        near_ref[i] = strip
        down_ref[pl.ds(body_rows + part * i, part), :] = strip[:part]
        up_ref[pl.ds(body_rows + part * i, part), :] = strip[STRIDE * (slab - TV_STEPS) :]


def smooth_kernel(nz, vol_ref, near_ref, low_ref, high_ref, out_ref, v, fz, fy, fx, turn):
    slab, rows, cols = vol_ref.shape
    body_rows = TV_STEPS * rows
    part = STRIDE * TV_STEPS
    depth = slab + 2 * TV_STEPS
    base = 16
    lane3 = lax.broadcasted_iota(jnp.int32, (TV_STEPS, cols), 1)
    first, last = lane_masks()
    turn[...] = jnp.zeros_like(turn)
    for z in range(depth):
        s = z - TV_STEPS
        if 0 <= s < slab:
            tile = vol_ref[s]
            near = [near_ref[i, pl.ds(STRIDE * s, TV_STEPS), :] for i in range(8)]
        else:
            src, k = (low_ref, z) if s < 0 else (high_ref, s - slab)
            tile = src[pl.ds(rows * k, rows), :]
            near = [src[pl.ds(body_rows + part * i + STRIDE * k, TV_STEPS), :] for i in range(8)]
        for half in range(2):
            v[z, half, pl.ds(0, base), :] = jnp.zeros((base, cols), jnp.float32)
            v[z, half, pl.ds(base + rows, 16), :] = jnp.zeros((16, cols), jnp.float32)
        v[z, 0, pl.ds(base, rows), :] = tile
        v[z, 0, pl.ds(base - TV_STEPS, TV_STEPS), :] = near[0]
        v[z, 0, pl.ds(base + rows, TV_STEPS), :] = near[1]
        for row, k in ((0, 2), (cols - TV_STEPS, 5)):
            above, beside, below = near[k : k + 3]
            ends = jnp.where(lane3 < 3 * cols // 4, pltpu.roll(below, rows, 1), pltpu.roll(above, rows, 1))
            turn[z, pl.ds(row, TV_STEPS), :] = jnp.where(lane3 < rows, beside, ends)
        sides = turn[z].T
        v[z, 1, pl.ds(base, rows), :] = sides[:rows]
        v[z, 1, pl.ds(base + rows, TV_STEPS), :] = sides[rows : rows + TV_STEPS]
        v[z, 1, pl.ds(base - TV_STEPS, TV_STEPS), :] = sides[cols - TV_STEPS :]

    z_first = lax.axis_index("angle") * slab - TV_STEPS + nz
    chunks = rows // 8 + 2
    for t in range(TV_STEPS):
        for z in range(t, depth - 1 - t):
            inner = jnp.where(lax.rem(z_first + z, nz) == nz - 1, 0.0, 1.0)
            for c in range(chunks - 1 if t == TV_STEPS - 1 else chunks):
                row = base - 8 + 8 * c
                mid = [v[z, half, pl.ds(row, 8), :] for half in range(2)]
                ahead = [pltpu.roll(m, cols - 1, 1) for m in mid]
                for half in range(2):
                    dz = (v[z + 1, half, pl.ds(row, 8), :] - mid[half]) * inner
                    dy = v[z, half, pl.ds(row + 1, 8), :] - mid[half]
                    dx = jnp.where(last, ahead[1 - half], ahead[half]) - mid[half]
                    scale = lax.rsqrt(dz * dz + dy * dy + dx * dx + tv_smooth * tv_smooth)
                    if half == 0 or t < TV_STEPS - 1:
                        fz[z, half, pl.ds(row, 8), :] = dz * scale
                        fy[z, half, pl.ds(row, 8), :] = dy * scale
                    fx[z, half, pl.ds(row, 8), :] = dx * scale

        for z in range(t + 1, depth - 1 - t):
            final = t == TV_STEPS - 1
            for c in range(1, chunks - 1) if final else range(chunks):
                row = base - 8 + 8 * c
                mid = [fx[z, half, pl.ds(row, 8), :] for half in range(2)]
                behind = [pltpu.roll(m, 1, 1) for m in mid]
                for half in range(1 if final else 2):
                    here = pl.ds(row, 8)
                    div = fz[z, half, here, :] - fz[z - 1, half, here, :]
                    div = div + (fy[z, half, here, :] - fy[z, half, pl.ds(row - 1, 8), :])
                    div = div + (mid[half] - jnp.where(first, behind[1 - half], behind[half]))
                    new = v[z, half, here, :] + tv_rate * div
                    if final:
                        out_ref[z - TV_STEPS, pl.ds(row - base, 8), :] = new
                    else:
                        v[z, half, here, :] = new


def step_and_smooth(parts, index, order, nz):
    slab, rows, cols = index.shape
    nx, ny = lax.axis_size("tx"), lax.axis_size("ty")
    block = jax.ShapeDtypeStruct(index.shape, jnp.float32)
    params = pltpu.CompilerParams(vmem_limit_bytes=40 * 2**20)
    strip_rows = STRIDE * slab
    gradient, volume, strips = pl.pallas_call(
        functools.partial(share_kernel, nx, ny),
        out_shape=(block, block, jax.ShapeDtypeStruct((nx * ny, strip_rows, cols), jnp.float32)),
        compiler_params=params,
        name="share",
    )(parts, index, order)
    strips = lax.all_to_all(strips, ("tx", "ty"), 0, 0, tiled=True)
    outward = jax.ShapeDtypeStruct((TV_STEPS * (rows + 8 * STRIDE), cols), jnp.float32)
    near, up, down = pl.pallas_call(
        functools.partial(sort_kernel, nx, ny),
        out_shape=(jax.ShapeDtypeStruct((8, strip_rows, cols), jnp.float32), outward, outward),
        compiler_params=params,
        name="sort",
    )(strips, volume)
    depth = lax.axis_size("angle")
    low = lax.ppermute(up, "angle", ring(depth, 1))
    high = lax.ppermute(down, "angle", ring(depth, -1))
    whole = pltpu.VMEM((slab + 2 * TV_STEPS, 2, rows + 32, cols), jnp.float32)
    smoothed = pl.pallas_call(
        functools.partial(smooth_kernel, nz),
        out_shape=block,
        scratch_shapes=[whole, whole, whole, whole, pltpu.VMEM((slab + 2 * TV_STEPS, cols, cols), jnp.float32)],
        compiler_params=params,
        name="smooth",
    )(volume, near, low, high)
    return gradient, smoothed


def body(index, measured, illum):
    slab, rows, cols = index.shape
    depth = lax.axis_size("angle")
    nz = slab * depth
    nx = cols * lax.axis_size("tx")
    ny = rows * lax.axis_size("ty")
    tall = 3 * rows
    chip_groups = [list(range(c, depth, 2)) for c in range(2)]

    block = (2, tall, cols)
    lane = lax.broadcasted_iota(jnp.int32, block, 2)
    column = 2 * lane + lax.broadcasted_iota(jnp.int32, block, 0)
    gx = lax.axis_index("tx") * cols + jnp.where(lane < cols - cols // 4, column, column - 2 * cols)
    gy = lax.axis_index("ty") * rows - rows + lax.broadcasted_iota(jnp.int32, block, 1)
    turns = (illum[0, 0] * gx * (ny // math.gcd(nx, ny)) + illum[0, 1] * gy * (nx // math.gcd(nx, ny)))
    whole = math.lcm(nx, ny)
    turns = lax.rem(lax.rem(turns, whole) + whole, whole)
    q = (2.0 * math.pi / whole) * turns.astype(jnp.float32)
    start = jnp.stack([jnp.cos(q), jnp.sin(q)])

    order = parity_order(cols)
    column = lax.all_gather(pack_corners(*widen(reorder(index, order), "tx", "ty")), "angle", axis=0, tiled=True)

    index_block = (GROUP, 5 * rows, cols)
    field_block = (GROUP, 2, rows, cols)
    steps = nz // GROUP
    scratch = [pltpu.VMEM((2, 4, tall + 16, cols), jnp.float32)]
    params = pltpu.CompilerParams(dimension_semantics=("arbitrary",), vmem_limit_bytes=40 * 2**20)
    fields = pl.pallas_call(
        functools.partial(forward_kernel, tall),
        grid=(steps,),
        in_specs=[
            pl.BlockSpec(index_block, lambda i: (i, 0, 0)),
            pl.BlockSpec((2, 2, tall, cols), lambda i: (0, 0, 0, 0)),
        ],
        out_specs=pl.BlockSpec(field_block, lambda i: (i, 0, 0, 0)),
        out_shape=jax.ShapeDtypeStruct((nz, 2, rows, cols), jnp.float32),
        scratch_shapes=scratch,
        compiler_params=params,
        name="forward",
    )(column, start)

    back = (TURN.conjugate() ** nz)
    back = back / abs(back)
    target = reorder(measured[:, 0], order)
    target_re = back.real * target[0] - back.imag * target[1]
    target_im = back.real * target[1] + back.imag * target[0]
    residual = fields[nz - 1] - jnp.stack([target_re, target_im])
    adjoint = jnp.concatenate(widen(residual, "tx", "ty"), axis=2)

    grads = pl.pallas_call(
        functools.partial(backward_kernel, tall),
        grid=(steps,),
        in_specs=[
            pl.BlockSpec(index_block, lambda i: (steps - 1 - i, 0, 0)),
            pl.BlockSpec((2, 2, tall, cols), lambda i: (0, 0, 0, 0)),
            pl.BlockSpec(field_block, lambda i: (steps - 1 - i, 0, 0, 0)),
        ],
        out_specs=pl.BlockSpec((2, 1, slab, rows, cols), lambda i: (0, steps - 1 - i, 0, 0, 0)),
        out_shape=jax.ShapeDtypeStruct((2, depth // 2, slab, rows, cols), jnp.float32),
        scratch_shapes=scratch + [pltpu.VMEM((4, rows, cols), jnp.float32)],
        compiler_params=params,
        name="backward",
    )(column, adjoint, fields)

    both = grads[0] + lax.ppermute(grads[1], "angle", [(i, i ^ 1) for i in range(depth)])
    parts = lax.all_to_all(both, "angle", 0, 0, tiled=True, axis_index_groups=chip_groups)
    return step_and_smooth(parts, index, order.T, nz)


def solution(mesh):
    in_specs = (P("angle", "ty", "tx"), P(None, "angle", "ty", "tx"), P("angle", None))
    out_specs = (P("angle", "ty", "tx"), P("angle", "ty", "tx"))
    return jax.shard_map(body, mesh=mesh, in_specs=in_specs, out_specs=out_specs, check_vma=False)
```

```python
import functools
import math

import jax
import jax.numpy as jnp
import numpy as np
from jax import lax
from jax.experimental import pallas as pl
from jax.experimental.pallas import tpu as pltpu
from jax.sharding import PartitionSpec as P

TV_STEPS = 3
HALO = 64
GROUP = 8

damping = 0.2
disperse = 0.1
phase_scale = 0.1
step_size = 0.1
tv_rate = 0.05
tv_smooth = 0.1

SPREAD = complex(damping, disperse)
GAIN = abs(SPREAD)
TURN = SPREAD / GAIN


def _fit():
    nodes = np.cos((np.arange(400) + 0.5) * np.pi / 400)
    t = 3.05 * (nodes + 1.0)
    z = t * t
    scaled = z / z.max()
    even = np.linalg.lstsq(scaled[:, None] ** np.arange(4), GAIN * np.cos(phase_scale * t), rcond=None)[0]
    odd = np.linalg.lstsq(scaled[:, None] ** np.arange(4), GAIN * np.sin(phase_scale * t) / t, rcond=None)[0]
    powers = z.max() ** np.arange(4)
    return [float(v) for v in even / powers], [float(v) for v in odd / powers]


EVEN, ODD = _fit()


def phase_factor(t):
    z = t * t
    cosine = EVEN[3]
    for coef in EVEN[2::-1]:
        cosine = cosine * z + coef
    sine = ODD[3]
    for coef in ODD[2::-1]:
        sine = sine * z + coef
    return cosine, sine * t


def neighbours(buf, slot, part, row):
    even, odd = [buf[slot, 2 * part + parity, pl.ds(row, 8), :] for parity in range(2)]
    sides = (odd + pltpu.roll(odd, 1, 1), even + pltpu.roll(even, 127, 1))
    out = []
    for parity in range(2):
        up = buf[slot, 2 * part + parity, pl.ds(row - 1, 8), :]
        down = buf[slot, 2 * part + parity, pl.ds(row + 1, 8), :]
        out.append(sides[parity] + (up + down))
    return (even, odd), out


def index_rows(index_ref, j, parity, c, chunks):
    third = chunks // 3
    rows = index_ref.shape[1] // 5
    if c < 2 * third:
        return index_ref[j, pl.ds(2 * rows * parity + 8 * c, 8), :]
    c = c - 2 * third
    corner = index_ref[j, pl.ds(2 * rows * parity + 8 * c, 8), :]
    own = index_ref[j, pl.ds(4 * rows + 8 * c, 8), :]
    if parity:
        own = pltpu.roll(own, 64, 1)
    lane = lax.broadcasted_iota(jnp.int32, (8, 128), 1)
    corner = jnp.where(lane < 96, pltpu.roll(corner, 96, 1), pltpu.roll(corner, 32, 1))
    return jnp.where(lane < 64, own, corner)


def both_parities(even, odd):
    lane = lax.broadcasted_iota(jnp.int32, (8, 128), 1)
    return jnp.where(lane < 64, even, pltpu.roll(odd, 64, 1))


def lane_masks():
    lane = lax.broadcasted_iota(jnp.int32, (8, 128), 1)
    return lane == 0, lane == 127


def forward_kernel(rows, index_ref, start_ref, field_ref, buf):
    chunks = rows // 8
    pid = pl.program_id(0)

    @pl.when(pid == 0)
    def _():
        buf[...] = jnp.zeros_like(buf)
        for q in range(4):
            buf[0, q, 8 : 8 + rows, :] = start_ref[q // 2, q % 2]

    def step(j, parity, lo, hi):
        for c in range(lo, hi):
            row = 8 + 8 * c
            re, sum_re = neighbours(buf, parity, 0, row)
            im, sum_im = neighbours(buf, parity, 1, row)
            for half in range(2):
                cosine, sine = phase_factor(index_rows(index_ref, j, half, c, chunks))
                wre = sum_re[half] + (im[half] + im[half])
                wim = sum_im[half] - (re[half] + re[half])
                nre = cosine * wre - sine * wim
                nim = cosine * wim + sine * wre
                buf[1 - parity, half, pl.ds(row, 8), :] = nre
                buf[1 - parity, 2 + half, pl.ds(row, 8), :] = nim
        for c in range(chunks // 3, 2 * chunks // 3):
            row = pl.ds(8 + 8 * c, 8)
            own = pl.ds(8 * (c - chunks // 3), 8)
            for part in range(2):
                even, odd = (buf[1 - parity, 2 * part + half, row, :] for half in range(2))
                field_ref[j, part, own, :] = both_parities(even, odd)

    for k in range(8):

        @pl.when(pid == k)
        def _(k=k):
            @pl.loop(0, GROUP // 2, unroll=2)
            def _(pair):
                step(2 * pair, 0, k, chunks - k)
                step(2 * pair + 1, 1, k, chunks - k)


def backward_kernel(rows, index_ref, start_ref, field_ref, grad_ref, buf, here):
    chunks = rows // 8
    pid = pl.program_id(0)
    core = lax.rem(lax.axis_index("angle"), 2)

    @pl.when(pid == 0)
    def _():
        buf[...] = jnp.zeros_like(buf)

    def finish(j, slot, c, are, aim):
        if chunks // 3 <= c < 2 * chunks // 3:
            own = pl.ds(8 * (c - chunks // 3), 8)
            for half in range(2):
                here[half, own, :] = are[half]
                here[2 + half, own, :] = aim[half]
        row = 8 + 8 * c
        for half in range(2):
            cosine, sine = phase_factor(index_rows(index_ref, j, half, c, chunks))
            buf[slot, half, pl.ds(row, 8), :] = cosine * are[half] + sine * aim[half]
            buf[slot, 2 + half, pl.ds(row, 8), :] = cosine * aim[half] - sine * are[half]

    def multiply(j):
        slab = GROUP // 2
        spot = lax.rem(j // slab + core, 2)
        for c in range(chunks // 3):
            own = pl.ds(8 * c, 8)
            are = both_parities(here[0, own, :], here[1, own, :])
            aim = both_parities(here[2, own, :], here[3, own, :])
            grad = aim * field_ref[j, 0, own, :] - are * field_ref[j, 1, own, :]
            grad_ref[spot, 0, j % slab, own, :] = phase_scale * grad

    def step(j, parity, lo, hi):
        for c in range(lo, hi):
            row = 8 + 8 * c
            re, sum_re = neighbours(buf, 1 - parity, 0, row)
            im, sum_im = neighbours(buf, 1 - parity, 1, row)
            are = [sum_re[half] - (im[half] + im[half]) for half in range(2)]
            aim = [sum_im[half] + (re[half] + re[half]) for half in range(2)]
            finish(j, parity, c, are, aim)
        multiply(j)

    for k in range(8):

        @pl.when(pid == k)
        def _(k=k):
            skip = 0
            if k == 0:
                skip = 1
                for c in range(chunks):
                    row = pl.ds(8 * c, 8)
                    finish(
                        GROUP - 1,
                        1,
                        c,
                        [start_ref[0, half, row, :] for half in range(2)],
                        [start_ref[1, half, row, :] for half in range(2)],
                    )
                multiply(GROUP - 1)
                step(GROUP - 2, 0, k, chunks - k)

            @pl.loop(skip, GROUP // 2, unroll=1 if skip else 2)
            def _(pair):
                step(GROUP - 1 - 2 * pair, 1, k, chunks - k)
                step(GROUP - 2 - 2 * pair, 0, k, chunks - k)


def ring(count, by):
    return [(i, (i + by) % count) for i in range(count)]


def parity_order(cols):
    order = np.concatenate([np.arange(0, cols, 2), np.arange(1, cols, 2)])
    return jnp.asarray(np.eye(cols, dtype=np.float32)[:, order])


def reorder(block, matrix):
    return lax.dot_general(block, matrix, (((block.ndim - 1,), (0,)), ((), ())), precision=lax.Precision.HIGHEST)


def widen(block, axis_x, axis_y):
    n, rows, cols = block.shape
    half, quarter = cols // 2, cols // 4
    nx, ny = lax.axis_size(axis_x), lax.axis_size(axis_y)
    side = lambda start: jnp.concatenate(
        [block[..., start : start + quarter], block[..., start + half : start + half + quarter]], axis=2
    )
    pack = lambda v: jnp.concatenate([v[: n // 2], v[n // 2 :]], axis=2)
    unpack = lambda v: jnp.concatenate([v[:, :, :half], v[:, :, half:]], axis=0)
    left = unpack(lax.ppermute(pack(side(quarter)), axis_x, ring(nx, 1)))
    right = unpack(lax.ppermute(pack(side(0)), axis_x, ring(nx, -1)))
    even = jnp.concatenate([block[..., :half], right[..., :quarter], left[..., :quarter]], axis=2)
    odd = jnp.concatenate([block[..., half:], right[..., quarter:], left[..., quarter:]], axis=2)
    wide = jnp.stack([even, odd], axis=1)
    above = lax.ppermute(wide, axis_y, ring(ny, 1))
    below = lax.ppermute(wide, axis_y, ring(ny, -1))
    return above, wide, below


def pack_corners(above, wide, below):
    n, _, rows, cols = wide.shape
    half, quarter = cols // 2, cols // 4
    lane = lax.broadcasted_iota(jnp.int32, (2, rows, cols), 2)
    parity = lax.broadcasted_iota(jnp.int32, (2, rows, cols), 0)
    away = jnp.where(lane < cols - quarter, 2 * (lane - half) + 1 + parity, 2 * (cols - lane) - parity)
    own = lane < half
    from_above = own | (away <= lax.broadcasted_iota(jnp.int32, (2, rows, cols), 1))
    swapped = jnp.concatenate([below[..., :half], below[..., cols - quarter :], below[..., half : cols - quarter]], axis=3)
    upper = jnp.concatenate([jnp.where(from_above, above, swapped), wide], axis=2).reshape(n, 4 * rows, cols)
    lower = jnp.concatenate([below[:, 0, :, :half], below[:, 1, :, :half]], axis=2)
    return jnp.concatenate([upper, lower], axis=1)


AROUND = [(0, -1), (0, 1), (1, -1), (1, 0), (1, 1), (-1, -1), (-1, 0), (-1, 1)]
STRIDE = 4


def tile_at(nx, ny, dx, dy):
    tx, ty = lax.axis_index("tx"), lax.axis_index("ty")
    return lax.rem(tx + dx + nx, nx) * ny + lax.rem(ty + dy + ny, ny)


def share_kernel(nx, ny, parts_ref, index_ref, order_ref, grad_ref, vol_ref, out_ref):
    slab, rows, cols = index_ref.shape
    out_ref[...] = jnp.zeros_like(out_ref)
    for s in range(slab):
        grad = parts_ref[0, s]
        for p in range(1, parts_ref.shape[0]):
            grad = grad + parts_ref[p, s]
        grad = jnp.dot(grad, order_ref[...], precision=lax.Precision.HIGHEST, preferred_element_type=jnp.float32)
        vol = index_ref[s] - step_size * grad
        grad_ref[s] = grad
        vol_ref[s] = vol
        turned = vol.T
        keep = pl.ds(STRIDE * s, TV_STEPS)
        for dx, dy in AROUND:
            spot = tile_at(nx, ny, dx, dy)
            if dx == 0:
                out_ref[spot, keep, :] = vol[rows - TV_STEPS :] if dy > 0 else vol[:TV_STEPS]
            else:
                out_ref[spot, keep, :rows] = turned[cols - TV_STEPS :] if dx > 0 else turned[:TV_STEPS]


def sort_kernel(nx, ny, strips_ref, vol_ref, near_ref, up_ref, down_ref):
    slab, rows, cols = vol_ref.shape
    body_rows = TV_STEPS * rows
    part = STRIDE * TV_STEPS
    for s in range(TV_STEPS):
        down_ref[pl.ds(rows * s, rows), :] = vol_ref[s]
        up_ref[pl.ds(rows * s, rows), :] = vol_ref[slab - TV_STEPS + s]
    for i, (dx, dy) in enumerate(AROUND):
        strip = strips_ref[tile_at(nx, ny, dx, dy)]
        near_ref[i] = strip
        down_ref[pl.ds(body_rows + part * i, part), :] = strip[:part]
        up_ref[pl.ds(body_rows + part * i, part), :] = strip[STRIDE * (slab - TV_STEPS) :]


def smooth_kernel(nz, vol_ref, near_ref, low_ref, high_ref, out_ref, v, fz, fy, fx, turn):
    slab, rows, cols = vol_ref.shape
    body_rows = TV_STEPS * rows
    part = STRIDE * TV_STEPS
    depth = slab + 2 * TV_STEPS
    base = 16
    lane3 = lax.broadcasted_iota(jnp.int32, (TV_STEPS, cols), 1)
    first, last = lane_masks()
    turn[...] = jnp.zeros_like(turn)
    for z in range(depth):
        s = z - TV_STEPS
        if 0 <= s < slab:
            tile = vol_ref[s]
            near = [near_ref[i, pl.ds(STRIDE * s, TV_STEPS), :] for i in range(8)]
        else:
            src, k = (low_ref, z) if s < 0 else (high_ref, s - slab)
            tile = src[pl.ds(rows * k, rows), :]
            near = [src[pl.ds(body_rows + part * i + STRIDE * k, TV_STEPS), :] for i in range(8)]
        for half in range(2):
            v[z, half, pl.ds(0, base), :] = jnp.zeros((base, cols), jnp.float32)
            v[z, half, pl.ds(base + rows, 16), :] = jnp.zeros((16, cols), jnp.float32)
        v[z, 0, pl.ds(base, rows), :] = tile
        v[z, 0, pl.ds(base - TV_STEPS, TV_STEPS), :] = near[0]
        v[z, 0, pl.ds(base + rows, TV_STEPS), :] = near[1]
        for row, k in ((0, 2), (cols - TV_STEPS, 5)):
            above, beside, below = near[k : k + 3]
            ends = jnp.where(lane3 < 3 * cols // 4, pltpu.roll(below, rows, 1), pltpu.roll(above, rows, 1))
            turn[z, pl.ds(row, TV_STEPS), :] = jnp.where(lane3 < rows, beside, ends)
        sides = turn[z].T
        v[z, 1, pl.ds(base, rows), :] = sides[:rows]
        v[z, 1, pl.ds(base + rows, TV_STEPS), :] = sides[rows : rows + TV_STEPS]
        v[z, 1, pl.ds(base - TV_STEPS, TV_STEPS), :] = sides[cols - TV_STEPS :]

    z_first = lax.axis_index("angle") * slab - TV_STEPS + nz
    chunks = rows // 8 + 2
    for t in range(TV_STEPS):
        for z in range(t, depth - 1 - t):
            inner = jnp.where(lax.rem(z_first + z, nz) == nz - 1, 0.0, 1.0)
            for c in range(chunks - 1 if t == TV_STEPS - 1 else chunks):
                row = base - 8 + 8 * c
                mid = [v[z, half, pl.ds(row, 8), :] for half in range(2)]
                ahead = [pltpu.roll(m, cols - 1, 1) for m in mid]
                for half in range(2):
                    dz = (v[z + 1, half, pl.ds(row, 8), :] - mid[half]) * inner
                    dy = v[z, half, pl.ds(row + 1, 8), :] - mid[half]
                    dx = jnp.where(last, ahead[1 - half], ahead[half]) - mid[half]
                    scale = lax.rsqrt(dz * dz + dy * dy + dx * dx + tv_smooth * tv_smooth)
                    if half == 0 or t < TV_STEPS - 1:
                        fz[z, half, pl.ds(row, 8), :] = dz * scale
                        fy[z, half, pl.ds(row, 8), :] = dy * scale
                    fx[z, half, pl.ds(row, 8), :] = dx * scale

        for z in range(t + 1, depth - 1 - t):
            final = t == TV_STEPS - 1
            for c in range(1, chunks - 1) if final else range(chunks):
                row = base - 8 + 8 * c
                mid = [fx[z, half, pl.ds(row, 8), :] for half in range(2)]
                behind = [pltpu.roll(m, 1, 1) for m in mid]
                for half in range(1 if final else 2):
                    here = pl.ds(row, 8)
                    div = fz[z, half, here, :] - fz[z - 1, half, here, :]
                    div = div + (fy[z, half, here, :] - fy[z, half, pl.ds(row - 1, 8), :])
                    div = div + (mid[half] - jnp.where(first, behind[1 - half], behind[half]))
                    new = v[z, half, here, :] + tv_rate * div
                    if final:
                        out_ref[z - TV_STEPS, pl.ds(row - base, 8), :] = new
                    else:
                        v[z, half, here, :] = new


def step_and_smooth(parts, index, order, nz):
    slab, rows, cols = index.shape
    nx, ny = lax.axis_size("tx"), lax.axis_size("ty")
    block = jax.ShapeDtypeStruct(index.shape, jnp.float32)
    params = pltpu.CompilerParams(vmem_limit_bytes=40 * 2**20)
    strip_rows = STRIDE * slab
    gradient, volume, strips = pl.pallas_call(
        functools.partial(share_kernel, nx, ny),
        out_shape=(block, block, jax.ShapeDtypeStruct((nx * ny, strip_rows, cols), jnp.float32)),
        compiler_params=params,
        name="share",
    )(parts, index, order)
    strips = lax.all_to_all(strips, ("tx", "ty"), 0, 0, tiled=True)
    outward = jax.ShapeDtypeStruct((TV_STEPS * (rows + 8 * STRIDE), cols), jnp.float32)
    near, up, down = pl.pallas_call(
        functools.partial(sort_kernel, nx, ny),
        out_shape=(jax.ShapeDtypeStruct((8, strip_rows, cols), jnp.float32), outward, outward),
        compiler_params=params,
        name="sort",
    )(strips, volume)
    depth = lax.axis_size("angle")
    low = lax.ppermute(up, "angle", ring(depth, 1))
    high = lax.ppermute(down, "angle", ring(depth, -1))
    whole = pltpu.VMEM((slab + 2 * TV_STEPS, 2, rows + 32, cols), jnp.float32)
    smoothed = pl.pallas_call(
        functools.partial(smooth_kernel, nz),
        out_shape=block,
        scratch_shapes=[whole, whole, whole, whole, pltpu.VMEM((slab + 2 * TV_STEPS, cols, cols), jnp.float32)],
        compiler_params=params,
        name="smooth",
    )(volume, near, low, high)
    return gradient, smoothed


def body(index, measured, illum):
    slab, rows, cols = index.shape
    depth = lax.axis_size("angle")
    nz = slab * depth
    nx = cols * lax.axis_size("tx")
    ny = rows * lax.axis_size("ty")
    tall = 3 * rows
    chip_groups = [list(range(c, depth, 2)) for c in range(2)]

    block = (2, tall, cols)
    lane = lax.broadcasted_iota(jnp.int32, block, 2)
    column = 2 * lane + lax.broadcasted_iota(jnp.int32, block, 0)
    gx = lax.axis_index("tx") * cols + jnp.where(lane < cols - cols // 4, column, column - 2 * cols)
    gy = lax.axis_index("ty") * rows - rows + lax.broadcasted_iota(jnp.int32, block, 1)
    turns = (illum[0, 0] * gx * (ny // math.gcd(nx, ny)) + illum[0, 1] * gy * (nx // math.gcd(nx, ny)))
    whole = math.lcm(nx, ny)
    turns = lax.rem(lax.rem(turns, whole) + whole, whole)
    q = (2.0 * math.pi / whole) * turns.astype(jnp.float32)
    start = jnp.stack([jnp.cos(q), jnp.sin(q)])

    order = parity_order(cols)
    column = lax.all_gather(pack_corners(*widen(reorder(index, order), "tx", "ty")), "angle", axis=0, tiled=True)

    index_block = (GROUP, 5 * rows, cols)
    field_block = (GROUP, 2, rows, cols)
    steps = nz // GROUP
    scratch = [pltpu.VMEM((2, 4, tall + 16, cols), jnp.float32)]
    params = pltpu.CompilerParams(dimension_semantics=("arbitrary",), vmem_limit_bytes=40 * 2**20)
    fields = pl.pallas_call(
        functools.partial(forward_kernel, tall),
        grid=(steps,),
        in_specs=[
            pl.BlockSpec(index_block, lambda i: (i, 0, 0)),
            pl.BlockSpec((2, 2, tall, cols), lambda i: (0, 0, 0, 0)),
        ],
        out_specs=pl.BlockSpec(field_block, lambda i: (i, 0, 0, 0)),
        out_shape=jax.ShapeDtypeStruct((nz, 2, rows, cols), jnp.float32),
        scratch_shapes=scratch,
        compiler_params=params,
        name="forward",
    )(column, start)

    back = (TURN.conjugate() ** nz)
    back = back / abs(back)
    target = reorder(measured[:, 0], order)
    target_re = back.real * target[0] - back.imag * target[1]
    target_im = back.real * target[1] + back.imag * target[0]
    residual = fields[nz - 1] - jnp.stack([target_re, target_im])
    adjoint = jnp.concatenate(widen(residual, "tx", "ty"), axis=2)

    grads = pl.pallas_call(
        functools.partial(backward_kernel, tall),
        grid=(steps,),
        in_specs=[
            pl.BlockSpec(index_block, lambda i: (steps - 1 - i, 0, 0)),
            pl.BlockSpec((2, 2, tall, cols), lambda i: (0, 0, 0, 0)),
            pl.BlockSpec(field_block, lambda i: (steps - 1 - i, 0, 0, 0)),
        ],
        out_specs=pl.BlockSpec((2, 1, slab, rows, cols), lambda i: (0, steps - 1 - i, 0, 0, 0)),
        out_shape=jax.ShapeDtypeStruct((2, depth // 2, slab, rows, cols), jnp.float32),
        scratch_shapes=scratch + [pltpu.VMEM((4, rows, cols), jnp.float32)],
        compiler_params=params,
        name="backward",
    )(column, adjoint, fields)

    both = grads[0] + lax.ppermute(grads[1], "angle", [(i, i ^ 1) for i in range(depth)])
    parts = lax.all_to_all(both, "angle", 0, 0, tiled=True, axis_index_groups=chip_groups)
    return step_and_smooth(parts, index, order.T, nz)


def solution(mesh):
    in_specs = (P("angle", "ty", "tx"), P(None, "angle", "ty", "tx"), P("angle", None))
    out_specs = (P("angle", "ty", "tx"), P("angle", "ty", "tx"))
    return jax.shard_map(body, mesh=mesh, in_specs=in_specs, out_specs=out_specs, check_vma=False)
```
